512 devices in a mesh: ctx: 64 (over z, y_lo, core), tp: 8 (over x, y_hi).
Axes of the slice: x: 4, y: 8 (y_hi: 2, y_lo: 4; y = y_hi * 4 + y_lo), z: 8, core: 2. Of those that a mesh axis runs over, the one named last changes fastest.
Arguments:
- projected: bfloat16 [3, 16384, 8192], P(None, 'ctx', 'tp'), may hold values from -6 to 6
- short_filter: float32 [3, 3, 8192], P(None, None, 'tp'), may hold values from -3.5 to 3.5
- decay_rate: float32 [8192, 16], P('tp'), may hold values from 6.1035156e-06 to 0.033, as said below
- residue: float32 [8192, 16], P('tp')
- skip_gain: float32 [8192], P('tp'), may hold values from -4 to 4
- out_weight: bfloat16 [8192, 4096], P(('tp', 'ctx')), may hold values from -0.25 to 0.25
Outputs:
- block_out: bfloat16 [16384, 4096], P('ctx', 'tp')
The draws below stay inside these ranges and needn't reach their ends.
Inputs may be any that keep to these rules, and one draw needn't show every extreme that they name: `decay_rate`: positive.
All inputs are finite; a program needn't handle non-finite values.
Results may differ from the reference program's by a relative error of at most 0.017.
Values may be sent and summed in bfloat16 or wider, within the bound.
A program may use at most 128 MiB of HBM per device.

```python
import math
import jax
import jax.numpy as jnp
from jax import lax

D = 8192
D_OUT = 4096
KSHORT = 3
STATES = 16
SEQ = 16384


def pole_rates(key, slow_share):
    key_unit, key_kind = jax.random.split(key)
    unit = jax.random.uniform(key_unit, (D, STATES), jnp.float32)
    slow = jax.random.bernoulli(key_kind, slow_share, (D, STATES))
    lower = jnp.where(slow, math.log(0.1 / SEQ), math.log(2.0 / SEQ))
    upper = jnp.where(slow, math.log(2.0 / SEQ), math.log(0.033))
    return jnp.exp(lower + unit * (upper - lower))


def draw_decay_rate(key, part):
    share = 0.5
    return pole_rates(key, share)


def draw_residue(key, part):
    share = 0.5
    rates = pole_rates(key, share)
    key = jax.random.fold_in(key, 7)
    spread = jax.random.normal(key, (D, STATES), jnp.float32)
    return spread * jnp.sqrt(2.0 * rates / STATES)


def raised(drawn, rng, source, target, blocks, factor):
    owner, partner = [(jnp.arange(drawn.shape[dim]) // (drawn.shape[dim] // blocks)).reshape([-1 if axis == dim else 1 for axis in range(drawn.ndim)]) for dim in (source, target)]
    chosen = jax.random.permutation(rng, blocks)[partner]
    strong = (owner == chosen) | (owner == (partner + blocks // 2) % blocks)
    return jnp.where(strong, factor * drawn, drawn)


def level_of(key, extent, pieces, least, top_value):
    def one(axis_at, parts):
        steps = jax.random.uniform(jax.random.fold_in(jax.random.fold_in(key, 6), axis_at), (parts,), jnp.float32, least / len(pieces), top_value / len(pieces))
        return jnp.repeat(jnp.exp(steps), extent[axis_at] // parts).reshape((-1,) + (1,) * (len(extent) - axis_at - 1))

    loudness = one(*pieces[0])
    for cut in pieces[1:]:
        loudness = loudness * one(*cut)
    return loudness


def scatter_about(stream_key, extent, scale, limit, pieces=(), held_as=jnp.bfloat16):
    result = jax.random.normal(stream_key, extent, jnp.float32) * scale
    if len(pieces) > 0:
        result = level_of(stream_key, extent, pieces, -0.22, 0.18) * result
    return jnp.clip(result, min=-limit, max=limit).astype(held_as)


def noise_with(stream_key, extent, width, bound, cuts, heavy, kind=jnp.bfloat16):
    result = width * jax.random.normal(stream_key, extent, jnp.float32)
    if cuts:
        result = result * level_of(stream_key, extent, cuts, -0.22, 0.18)
    return jnp.clip(raised(result, jax.random.fold_in(stream_key, 3), *heavy), -bound, bound).astype(kind)


def setup_inputs(seed: int = 0) -> dict:
    arg_keys = jax.random.split(jax.random.key(seed), 7)
    projected = scatter_about(arg_keys[0], (3, SEQ, D), 1.0, 6.0, ((1, 64), (2, 8)))
    short_filter = scatter_about(arg_keys[1], (3, KSHORT, D), KSHORT ** -0.5, 3.5, ((2, 8),), jnp.float32)
    decay_rate = draw_decay_rate(jax.random.fold_in(arg_keys[6], 71), 0)
    residue = draw_residue(jax.random.fold_in(arg_keys[6], 71), 0)
    skip_gain = scatter_about(arg_keys[4], (D,), 1.0, 4.0, ((0, 8),), jnp.float32)
    out_weight = noise_with(arg_keys[5], (D, D_OUT), D ** -0.5, 0.25, ((0, 512),), (0, 1, 512, 6.0))
    return {"projected": projected, "short_filter": short_filter, "decay_rate": decay_rate, "residue": residue, "skip_gain": skip_gain, "out_weight": out_weight}


def causal_filter(gated_block, rate_block, weight_block):
    seq_len = gated_block.shape[0]
    times = jnp.arange(seq_len, dtype=jnp.float32)[:, None]
    impulse = jnp.zeros(gated_block.shape, jnp.float32)
    for pole_index in range(rate_block.shape[1]):
        impulse = impulse + weight_block[:, pole_index][None, :] * jnp.exp(-rate_block[:, pole_index][None, :] * times)
    total_len = 2 * seq_len
    spectrum = jnp.fft.rfft(gated_block.astype(jnp.float32), n=total_len, axis=0) * jnp.fft.rfft(impulse, n=total_len, axis=0)
    return jnp.fft.irfft(spectrum, n=total_len, axis=0)[:seq_len]


def reference(projected, short_filter, decay_rate, residue, skip_gain, out_weight):
    block_width = min(D, 512)
    taps = KSHORT
    block_count = D // block_width

    def one_block(total, block_index):
        start = (block_index * block_width).astype(jnp.int32)
        piece = lax.dynamic_slice_in_dim(projected, start, block_width, 2).astype(jnp.float32)
        taps_part = lax.dynamic_slice_in_dim(short_filter, start, block_width, 2)
        padded = jnp.pad(piece, ((0, 0), (taps - 1, 0), (0, 0)))
        featured = jnp.zeros(piece.shape, jnp.float32)
        for tap_index in range(taps):
            featured = featured + taps_part[:, tap_index:tap_index + 1, :] * padded[:, taps - 1 - tap_index:taps - 1 - tap_index + SEQ, :]
        gated = (featured[1] * featured[2]).astype(jnp.bfloat16)
        rates = lax.dynamic_slice_in_dim(decay_rate, start, block_width, 0)
        weights = lax.dynamic_slice_in_dim(residue, start, block_width, 0)
        gains = lax.dynamic_slice_in_dim(skip_gain, start, block_width, 0)
        filtered = (causal_filter(gated, rates, weights) + gains[None, :] * gated.astype(jnp.float32)).astype(jnp.bfloat16)
        mixed = (featured[0] * filtered.astype(jnp.float32)).astype(jnp.bfloat16)
        rows_part = lax.dynamic_slice_in_dim(out_weight, start, block_width, 0)
        return total + jnp.dot(mixed, rows_part, preferred_element_type=jnp.float32), None

    total, _ = lax.scan(one_block, jnp.zeros((SEQ, D_OUT), jnp.float32), jnp.arange(block_count, dtype=jnp.int32))
    return total.astype(jnp.bfloat16)
```

```python
import jax
import jax.numpy as jnp
from jax import lax
from jax.experimental import pallas as pl
from jax.experimental.pallas import tpu as pltpu
from jax.sharding import PartitionSpec as P

ZS = 8
PLANE = 8
XS = 4
TOK = 256
CHAN = 1024
LANES = 128
GROUPS = CHAN // LANES
MODES = 16
ROWS = 16
BLOCK = PLANE * ROWS
PIECE = 256
UNROLL = 8


def block_kernel(
    proj,
    filt,
    rate,
    resid,
    skip,
    weight,
    out,
    wq,
    wbuf,
    halo_out,
    halo_in,
    gates,
    query,
    conv,
    decay,
    gain,
    power,
    state,
    stage1,
    total,
    stage2,
    carries,
    carry,
    mixed,
    far_out,
    up_out,
    down_out,
    far_up_in,
    far_down_in,
    up_in,
    down_in,
    half_out,
    half_in,
    halo_sem,
    wy_send,
    wy_recv,
    up_send,
    up_recv,
    dn_send,
    dn_recv,
    s1_send,
    s1_recv,
    s2_send,
    s2_recv,
    s3_send,
    s3_recv,
    mix_send,
    mix_recv,
    x_send,
    x_recv,
    h_send,
    h_recv,
):
    ctx = lax.axis_index("ctx")
    tp = lax.axis_index("tp")
    z = ctx // PLANE
    e = ctx % PLANE
    c = e % 2
    par = (e // 2) % 2
    quad = e // 4
    x = tp // 2
    h = tp % 2

    def at(zz, ee):
        return zz * PLANE + ee

    def member(pp, cc):
        return z * PLANE + quad * 4 + pp * 2 + cc

    def remote(src, dst, send, recv, to_ctx, to_tp):
        return pltpu.make_async_remote_copy(
            src_ref=src,
            dst_ref=dst,
            send_sem=send,
            recv_sem=recv,
            device_id={"ctx": to_ctx, "tp": to_tp},
            device_id_type=pl.DeviceIdType.MESH,
        )

    sent = []

    def start(*args):
        copy = remote(*args)
        copy.start()
        sent.append(copy)

    def arrived(dst, recv):
        remote(dst, dst, recv, recv, at((z + 1) % ZS, e), tp).wait_recv()

    barrier = pltpu.get_barrier_semaphore()

    def greet(to_ctx, to_tp):
        pl.semaphore_signal(
            barrier,
            inc=1,
            device_id={"ctx": to_ctx, "tp": to_tp},
            device_id_type=pl.DeviceIdType.MESH,
        )

    for k in range(1, PLANE):
        greet(at(z, (e + k) % PLANE), tp)
    for k in range(1, ZS):
        greet(at((z + k) % ZS, e), tp)
    for k in (1, XS - 1):
        greet(ctx, ((x + k) % XS) * 2 + h)
    for pp in range(2):
        for cc in range(2):
            greet(member(pp, cc), x * 2 + (1 - h))
    to_next = jnp.logical_and(e == PLANE - 1, z < ZS - 1)
    to_prev = jnp.logical_and(e == 0, z > 0)

    @pl.when(to_next)
    def _():
        greet(ctx + 1, tp)

    @pl.when(to_prev)
    def _():
        greet(ctx - 1, tp)

    for q in range(4):
        pp, cc = q // 2, q % 2
        for xx in range(XS):
            col = xx * 1024 + pp * 512 + cc * PIECE
            wq[q, :, xx * PIECE : (xx + 1) * PIECE] = weight[:, col : col + PIECE]
    rims = [proj[p, TOK - 16 : TOK, :].astype(jnp.float32)[14:16, :] for p in range(3)]
    for p in range(3):
        halo_out[2 * p : 2 * p + 2, :] = rims[p]
    halo_out[6:8, :] = jnp.zeros((2, CHAN), jnp.float32)

    @pl.when(ctx == 0)
    def _():
        halo_in[...] = jnp.zeros_like(halo_in)

    for g in range(GROUPS):
        cols = slice(g * LANES, (g + 1) * LANES)
        decay[pl.ds(g, MODES, stride=GROUPS), :] = jnp.exp(-rate[:, cols])
        power[pl.ds(g, MODES, stride=GROUPS), :] = rate[:, cols]
        gain[pl.ds(g, MODES, stride=GROUPS), :] = resid[:, cols]

    row_id = lax.broadcasted_iota(jnp.int32, (TOK, LANES), 0)

    def featurize(g, carry_in):
        lo = pl.multiple_of(g * LANES, LANES)
        cols = pl.ds(lo, LANES)
        featured = []
        for p in range(3):
            now = proj[p, :, cols].astype(jnp.float32)
            taps = filt[p, :, cols]
            one = jnp.where(row_id >= 1, pltpu.roll(now, 1, 0), 0.0)
            two = jnp.where(row_id >= 2, pltpu.roll(now, 2, 0), 0.0)
            featured.append(taps[0:1, :] * now + taps[1:2, :] * one + taps[2:3, :] * two)
        query[:, cols] = featured[0]
        gates[pl.ds(pl.multiple_of(g * TOK, TOK), TOK), :] = (
            (featured[1] * featured[2]).astype(jnp.bfloat16).astype(jnp.float32)
        )
        return carry_in

    lax.fori_loop(0, GROUPS, featurize, 0)

    beyond = jnp.logical_or(to_next, to_prev).astype(jnp.int32)
    pl.semaphore_wait(barrier, 7 + 7 + 2 + 4 + beyond)

    halo_copy = remote(halo_out, halo_in, halo_sem.at[0], halo_sem.at[1], ctx + 1, tp)

    @pl.when(ctx < ZS * PLANE - 1)
    def _():
        halo_copy.start()

    my_rows = pl.ds(pl.multiple_of(z * BLOCK + e * ROWS, ROWS), ROWS)
    for k in range(1, PLANE):
        ee = (e + k) % PLANE
        share = ((ee // 2) % 2) * 2 + ee % 2
        start(wq.at[share], wbuf.at[my_rows], wy_send.at[k], wy_recv.at[k], at(z, ee), tp)
    wbuf[my_rows, :] = wq[par * 2 + c]

    @pl.when(ctx > 0)
    def _():
        remote(halo_in, halo_in, halo_sem.at[0], halo_sem.at[1], ctx - 1, tp).wait_recv()

    edge_id = lax.broadcasted_iota(jnp.int32, (8, CHAN), 0)
    featured = []
    for p in range(3):
        now = proj[p, 0:16, :].astype(jnp.float32)[0:8, :]
        before2 = halo_in[2 * p : 2 * p + 1, :]
        before1 = halo_in[2 * p + 1 : 2 * p + 2, :]
        one = jnp.where(edge_id >= 1, pltpu.roll(now, 1, 0), before1)
        two = jnp.where(
            edge_id >= 2, pltpu.roll(now, 2, 0), jnp.where(edge_id == 0, before2, before1)
        )
        taps = filt[p]
        featured.append(taps[0:1, :] * now + taps[1:2, :] * one + taps[2:3, :] * two)
    query[0:8, :] = featured[0]
    first = (featured[1] * featured[2]).astype(jnp.bfloat16).astype(jnp.float32)
    for g in range(GROUPS):
        gates[g * TOK : g * TOK + 8, :] = first[:, g * LANES : (g + 1) * LANES]

    def token(ref, t):
        return ref[pl.ds(t, GROUPS, stride=TOK), :]

    def mode(ref, n):
        return ref[n * GROUPS : (n + 1) * GROUPS, :]

    zero = tuple(jnp.zeros((GROUPS, LANES), jnp.float32) for _ in range(MODES))

    def end_state(step, held):
        for u in range(UNROLL):
            g_now = token(gates, step * UNROLL + u)
            held = tuple(mode(decay, n) * held[n] + g_now for n in range(MODES))
        return held

    final = lax.fori_loop(0, TOK // UNROLL, end_state, zero)
    for n in range(MODES):
        state[n * GROUPS : (n + 1) * GROUPS, :] = final[n]

    own_modes = pl.ds(pl.multiple_of(e * 16, 16), 16)
    for k in range(1, PLANE):
        ee = (e + k) % PLANE
        start(
            state.at[pl.ds(pl.multiple_of(ee * 16, 16), 16)],
            stage1.at[e],
            s1_send.at[k],
            s1_recv.at[k],
            at(z, ee),
            tp,
        )
    stage1[e] = state[own_modes, :]

    for k in range(1, PLANE):
        ee = (e + PLANE - k) % PLANE
        arrived(
            wbuf.at[pl.ds(pl.multiple_of(z * BLOCK + ee * ROWS, ROWS), ROWS)], wy_recv.at[k]
        )
    half = BLOCK // 2

    def piece(zz, second):
        return wbuf.at[pl.ds(pl.multiple_of(zz * BLOCK + second * half, half), half)]

    def ring_wait(m):
        s = m // 2
        arrived(piece((z + 2 * ZS - 1 - s) % ZS, m % 2), up_recv.at[m])
        arrived(piece((z + 1 + s) % ZS, 1 - m % 2), dn_recv.at[m])

    def ring_send(m):
        if m >= 2:
            ring_wait(m - 2)
        s = m // 2
        up = piece((z + ZS - s) % ZS, m % 2)
        start(up, up, up_send.at[m], up_recv.at[m], at((z + 1) % ZS, e), tp)
        down = piece((z + s) % ZS, 1 - m % 2)
        start(down, down, dn_send.at[m], dn_recv.at[m], at((z + ZS - 1) % ZS, e), tp)

    ring_send(0)
    ring_send(1)

    def local_filter(step, held):
        for u in range(UNROLL):
            t = step * UNROLL + u
            g_now = token(gates, t)
            held = tuple(mode(decay, n) * held[n] + g_now for n in range(MODES))
            terms = [mode(gain, n) * held[n] for n in range(MODES)]
            terms.append(skip[...] * g_now)
            while len(terms) > 1:
                terms = [
                    terms[i] + terms[i + 1] if i + 1 < len(terms) else terms[i]
                    for i in range(0, len(terms), 2)
                ]
            conv[pl.ds(t, GROUPS, stride=TOK), :] = terms[0]
        return held

    steps = TOK // UNROLL
    held = lax.fori_loop(0, steps // 2, local_filter, zero)

    for k in range(1, PLANE):
        arrived(stage1.at[(e + PLANE - k) % PLANE], s1_recv.at[k])
    rates = power[own_modes, :]
    over_device = jnp.exp(rates * (-float(TOK)))
    over_plane = jnp.exp(rates * (-float(TOK * PLANE)))
    running = stage1[0]
    for k in range(1, PLANE):
        running = over_device * running + stage1[k]
    total[...] = running
    for k in range(1, ZS):
        start(total, stage2.at[z], s2_send.at[k], s2_recv.at[k], at((z + k) % ZS, e), tp)
    stage2[z] = running

    held = lax.fori_loop(steps // 2, steps, local_filter, held)

    for k in range(1, ZS):
        arrived(stage2.at[(z + ZS - k) % ZS], s2_recv.at[k])
    running = jnp.zeros((16, LANES), jnp.float32)
    for k in range(ZS - 1):
        running = jnp.where(k < z, over_plane * running + stage2[k], running)
    for k in range(PLANE):
        carries[k] = running
        if k < PLANE - 1:
            running = over_device * running + stage1[k]
    for k in range(1, PLANE):
        ee = (e + k) % PLANE
        start(carries.at[ee], carry.at[own_modes], s3_send.at[k], s3_recv.at[k], at(z, ee), tp)
    carry[own_modes, :] = carries[e]

    ring_send(2)
    ring_send(3)

    for k in range(1, PLANE):
        ee = (e + PLANE - k) % PLANE
        arrived(carry.at[pl.ds(pl.multiple_of(ee * 16, 16), 16)], s3_recv.at[k])

    def add_carry(step, held):
        for u in range(UNROLL):
            t = step * UNROLL + u
            held = tuple(mode(decay, n) * held[n] for n in range(MODES))
            terms = list(held) + [token(conv, t)]
            while len(terms) > 1:
                terms = [
                    terms[i] + terms[i + 1] if i + 1 < len(terms) else terms[i]
                    for i in range(0, len(terms), 2)
                ]
            conv[pl.ds(t, GROUPS, stride=TOK), :] = terms[0]
        return held

    lax.fori_loop(
        0, steps, add_carry, tuple(mode(gain, n) * mode(carry, n) for n in range(MODES))
    )

    def token_rows(pp, cc):
        return pl.ds(pl.multiple_of((pp * 2 + cc) * TOK, TOK), TOK)

    mine = token_rows(par, c)

    def mix(g, carry_in):
        cols = pl.ds(pl.multiple_of(g * LANES, LANES), LANES)
        filtered = conv[pl.ds(pl.multiple_of(g * TOK, TOK), TOK), :].astype(jnp.bfloat16)
        mixed[mine, cols] = (query[:, cols] * filtered.astype(jnp.float32)).astype(jnp.bfloat16)
        return carry_in

    lax.fori_loop(0, GROUPS, mix, 0)

    start(mixed.at[mine], mixed.at[mine], mix_send.at[0], mix_recv.at[0], member(par, 1 - c), tp)
    start(mixed.at[mine], mixed.at[mine], mix_send.at[1], mix_recv.at[1], member(1 - par, c), tp)

    ring_send(4)
    ring_send(5)
    across = token_rows(1 - par, c)
    arrived(mixed.at[across], mix_recv.at[1])
    start(
        mixed.at[across], mixed.at[across], mix_send.at[2], mix_recv.at[2], member(par, 1 - c), tp
    )
    ring_send(6)
    ring_wait(5)
    ring_wait(6)
    arrived(mixed.at[token_rows(par, 1 - c)], mix_recv.at[0])

    def product(m, d):
        rows = pl.ds(pl.multiple_of((par + m) % 2 * 512, 512), 512)
        cols = pl.ds(pl.multiple_of((x + d) % XS * PIECE, PIECE), PIECE)
        return jnp.dot(mixed[rows, :], wbuf[:, cols], preferred_element_type=jnp.float32)

    right = ((x + 1) % XS) * 2 + h
    left = ((x + XS - 1) % XS) * 2 + h
    upper, lower = pl.ds(0, TOK), pl.ds(TOK, TOK)

    def sends_over_x(m):
        far_out[m] = product(m, 2).astype(jnp.bfloat16)
        start(far_out.at[m, upper], far_up_in.at[m], x_send.at[m, 0], x_recv.at[m, 0], ctx, right)
        start(far_out.at[m, lower], far_down_in.at[m], x_send.at[m, 1], x_recv.at[m, 1], ctx, left)
        term = product(m, 1)
        up_out[m, lower] = term[TOK:].astype(jnp.bfloat16)
        arrived(far_up_in.at[m], x_recv.at[m, 0])
        up_out[m, upper] = (term[:TOK] + far_up_in[m].astype(jnp.float32)).astype(jnp.bfloat16)
        start(up_out.at[m], up_in.at[m], x_send.at[m, 2], x_recv.at[m, 2], ctx, right)
        term = product(m, 3)
        down_out[m, upper] = term[:TOK].astype(jnp.bfloat16)
        arrived(far_down_in.at[m], x_recv.at[m, 1])
        down_out[m, lower] = (term[TOK:] + far_down_in[m].astype(jnp.float32)).astype(jnp.bfloat16)
        start(down_out.at[m], down_in.at[m], x_send.at[m, 3], x_recv.at[m, 3], ctx, left)

    def sums_over_x(m):
        term = product(m, 0)
        arrived(up_in.at[m], x_recv.at[m, 2])
        arrived(down_in.at[m], x_recv.at[m, 3])
        both = up_in[m].astype(jnp.float32) + down_in[m].astype(jnp.float32)
        half_out[m] = (term + both).astype(jnp.bfloat16)
        for k in range(2):
            cc = (c + k) % 2
            rows = pl.ds(pl.multiple_of(cc * TOK, TOK), TOK)
            own_place = jnp.logical_and(m == 0 and k == 0, h == par)
            copy = remote(
                half_out.at[m, rows],
                half_in.at[h, c],
                h_send.at[m, k],
                h_recv.at[h, c],
                member((par + m) % 2, cc),
                x * 2 + par,
            )
            if m == 0 and k == 0:

                @pl.when(own_place)
                def _():
                    half_in[h, c] = half_out[m, rows]

                @pl.when(jnp.logical_not(own_place))
                def _():
                    copy.start()
            else:
                copy.start()
            last.append((copy, own_place if m == 0 and k == 0 else None))

    last = []
    sends_over_x(0)
    arrived(mixed.at[token_rows(1 - par, 1 - c)], mix_recv.at[2])
    sends_over_x(1)
    sums_over_x(0)
    sums_over_x(1)

    for a in range(2):
        for b in range(2):
            hs, cs = (h + a) % 2, (c + b) % 2
            if a == 0 and b == 0:

                @pl.when(par != h)
                def _():
                    arrived(half_in.at[hs, cs], h_recv.at[hs, cs])
            else:
                arrived(half_in.at[hs, cs], h_recv.at[hs, cs])
    for cs in range(2):
        out[:, cs * PIECE : (cs + 1) * PIECE] = (
            half_in[0, cs].astype(jnp.float32) + half_in[1, cs].astype(jnp.float32)
        ).astype(jnp.bfloat16)

    @pl.when(ctx < ZS * PLANE - 1)
    def _():
        halo_copy.wait_send()

    for copy in sent:
        copy.wait_send()
    for copy, own_place in last:
        if own_place is None:
            copy.wait_send()
        else:

            @pl.when(jnp.logical_not(own_place))
            def _():
                copy.wait_send()


def on_device(projected, short_filter, decay_rate, residue, skip_gain, out_weight):
    f32, bf16 = jnp.float32, jnp.bfloat16
    dma = pltpu.SemaphoreType.DMA
    scratch = [
        pltpu.VMEM((4, ROWS, 4 * PIECE), bf16),
        pltpu.VMEM((CHAN, 4 * PIECE), bf16),
        pltpu.VMEM((8, CHAN), f32),
        pltpu.VMEM((8, CHAN), f32),
        pltpu.VMEM((GROUPS * TOK, LANES), f32),
        pltpu.VMEM((TOK, CHAN), f32),
        pltpu.VMEM((GROUPS * TOK, LANES), f32),
        pltpu.VMEM((MODES * GROUPS, LANES), f32),
        pltpu.VMEM((MODES * GROUPS, LANES), f32),
        pltpu.VMEM((MODES * GROUPS, LANES), f32),
        pltpu.VMEM((MODES * GROUPS, LANES), f32),
        pltpu.VMEM((PLANE, 16, LANES), f32),
        pltpu.VMEM((16, LANES), f32),
        pltpu.VMEM((ZS, 16, LANES), f32),
        pltpu.VMEM((PLANE, 16, LANES), f32),
        pltpu.VMEM((MODES * GROUPS, LANES), f32),
        pltpu.VMEM((4 * TOK, CHAN), bf16),
        pltpu.VMEM((2, 2 * TOK, PIECE), bf16),
        pltpu.VMEM((2, 2 * TOK, PIECE), bf16),
        pltpu.VMEM((2, 2 * TOK, PIECE), bf16),
        pltpu.VMEM((2, TOK, PIECE), bf16),
        pltpu.VMEM((2, TOK, PIECE), bf16),
        pltpu.VMEM((2, 2 * TOK, PIECE), bf16),
        pltpu.VMEM((2, 2 * TOK, PIECE), bf16),
        pltpu.VMEM((2, 2 * TOK, PIECE), bf16),
        pltpu.VMEM((2, 2, TOK, PIECE), bf16),
        dma((2,)),
        dma((PLANE,)),
        dma((PLANE,)),
        dma((7,)),
        dma((7,)),
        dma((7,)),
        dma((7,)),
        dma((PLANE,)),
        dma((PLANE,)),
        dma((ZS,)),
        dma((ZS,)),
        dma((PLANE,)),
        dma((PLANE,)),
        dma((3,)),
        dma((3,)),
        dma((2, 4)),
        dma((2, 4)),
        dma((2, 2)),
        dma((2, 2)),
    ]
    return pl.pallas_call(
        block_kernel,
        out_shape=jax.ShapeDtypeStruct((TOK, 2 * PIECE), bf16),
        in_specs=[pl.BlockSpec(memory_space=pltpu.VMEM)] * 6,
        out_specs=pl.BlockSpec(memory_space=pltpu.VMEM),
        scratch_shapes=scratch,
        compiler_params=pltpu.CompilerParams(
            collective_id=0, has_side_effects=True, vmem_limit_bytes=40 * 1024 * 1024
        ),
    )(
        projected,
        short_filter,
        decay_rate.T,
        residue.T,
        skip_gain.reshape(GROUPS, LANES),
        out_weight,
    )


def solution(mesh):
    in_specs = (
        P(None, "ctx", "tp"),
        P(None, None, "tp"),
        P("tp", None),
        P("tp", None),
        P("tp"),
        P(("tp", "ctx"), None),
    )
    out_specs = P("ctx", "tp")
    return jax.shard_map(
        on_device, mesh=mesh, in_specs=in_specs, out_specs=out_specs, check_vma=False
    )
```

```python
import jax
import jax.numpy as jnp
from jax import lax
from jax.experimental import pallas as pl
from jax.experimental.pallas import tpu as pltpu
from jax.sharding import PartitionSpec as P

ZS = 8
PLANE = 8
XS = 4
TOK = 256
CHAN = 1024
LANES = 128
GROUPS = CHAN // LANES
MODES = 16
ROWS = 16
BLOCK = PLANE * ROWS
ORDER = (2, 1, 3, 0)
PIECE = 256
HEAD = 8
PARTS = ((0, 128), (128, 64), (192, 64))


def block_kernel(
    proj_hbm,
    filt_hbm,
    rate_hbm,
    resid_hbm,
    skip_hbm,
    weight_hbm,
    out,
    proj,
    filt,
    rate,
    resid,
    skip,
    weight,
    wq,
    wbuf,
    halo_out,
    halo_in,
    gates,
    query,
    conv,
    decay,
    gain,
    power,
    late,
    head,
    state,
    stage1,
    total,
    stage2,
    carries,
    carry,
    mixed,
    far_out,
    up_out,
    down_out,
    far_in,
    up_in,
    down_in,
    half_out,
    stay_sem,
    load_sem,
    halo_send,
    halo_recv,
    wy_send,
    wy_recv,
    up_send,
    up_recv,
    dn_send,
    dn_recv,
    s1_send,
    s1_recv,
    s2_send,
    s2_recv,
    s3_send,
    s3_recv,
    mix_send,
    mix_recv,
    x_send,
    x_recv,
    h_send,
    h_recv,
):
    ctx = lax.axis_index("ctx")
    tp = lax.axis_index("tp")
    z = ctx // PLANE
    e = ctx % PLANE
    c = e % 2
    par = (e // 2) % 2
    quad = e // 4
    x = tp // 2
    h = tp % 2

    def at(zz, ee):
        return zz * PLANE + ee

    def partner(k):
        return ((e // 4 + k // 4) % 2) * 4 + ((e // 2 + k // 2) % 2) * 2 + (e + k) % 2

    def member(pp, cc):
        return z * PLANE + quad * 4 + pp * 2 + cc

    def remote(src, dst, send, recv, to_ctx, to_tp):
        return pltpu.make_async_remote_copy(
            src_ref=src,
            dst_ref=dst,
            send_sem=send,
            recv_sem=recv,
            device_id={"ctx": to_ctx, "tp": to_tp},
            device_id_type=pl.DeviceIdType.MESH,
        )

    sent = []

    def start(*args):
        copy = remote(*args)
        copy.start()
        sent.append(copy)

    def arrived(dst, recv):
        remote(dst, dst, recv, recv, at((z + 1) % ZS, e), tp).wait_recv()

    barrier = pltpu.get_barrier_semaphore()

    def greet(to_ctx, to_tp):
        pl.semaphore_signal(
            barrier,
            inc=1,
            device_id={"ctx": to_ctx, "tp": to_tp},
            device_id_type=pl.DeviceIdType.MESH,
        )

    for k in range(1, PLANE):
        greet(at(z, (e + k) % PLANE), tp)
    for k in range(1, ZS):
        greet(at((z + k) % ZS, e), tp)
    for k in (1, XS - 1):
        greet(ctx, ((x + k) % XS) * 2 + h)
    for pp in range(2):
        for cc in range(2):
            greet(member(pp, cc), x * 2 + (1 - h))
    to_next = jnp.logical_and(e == PLANE - 1, z < ZS - 1)
    to_prev = jnp.logical_and(e == 0, z > 0)

    @pl.when(to_next)
    def _():
        greet(ctx + 1, tp)

    @pl.when(to_prev)
    def _():
        greet(ctx - 1, tp)

    loads = [
        pltpu.make_async_copy(src, dst, load_sem.at[k])
        for k, (src, dst) in enumerate(
            [
                (weight_hbm, weight),
                (proj_hbm.at[1], proj.at[1]),
                (proj_hbm.at[2], proj.at[2]),
                (proj_hbm.at[0], proj.at[0]),
                (rate_hbm, rate),
                (filt_hbm, filt),
                (resid_hbm, resid),
                (skip_hbm, skip),
            ]
        )
    ]
    for copy in loads:
        copy.start()

    loads[0].wait()
    for q in range(4):
        pp, cc = q // 2, q % 2
        for j in range(XS):
            col = (x + ORDER[j]) % XS * 1024 + pp * 512 + cc * PIECE
            wq[q, j] = weight[:, pl.ds(pl.multiple_of(col, PIECE), PIECE)]
    for k in range(1, 4):
        loads[k].wait()
    for p in range(3):
        rim = proj[p, TOK - 16 : TOK, :].astype(jnp.float32)
        halo_out[2 * p : 2 * p + 2, :] = rim[14:16, :]
    halo_out[6:8, :] = jnp.zeros((2, CHAN), jnp.float32)

    @pl.when(ctx == 0)
    def _():
        halo_in[...] = jnp.zeros_like(halo_in)

    beyond = jnp.logical_or(to_next, to_prev).astype(jnp.int32)
    pl.semaphore_wait(barrier, 7 + 7 + 2 + 4 + beyond)

    halo_copy = remote(halo_out, halo_in, halo_send.at[0], halo_recv.at[0], ctx + 1, tp)

    @pl.when(ctx < ZS * PLANE - 1)
    def _():
        halo_copy.start()

    my_rows = pl.ds(pl.multiple_of(z * BLOCK + e * ROWS, ROWS), ROWS)
    for group in range(2):
        js = pl.ds(2 * group, 2)
        for k in range(1, PLANE):
            ee = partner(k)
            share = ((ee // 2) % 2) * 2 + ee % 2
            start(
                wq.at[share, js],
                wbuf.at[js, my_rows],
                wy_send.at[group, k],
                wy_recv.at[group, k],
                at(z, ee),
                tp,
            )
    wbuf[:, my_rows, :] = wq[par * 2 + c]

    def piece(zz, j):
        return wbuf.at[j, pl.ds(pl.multiple_of(zz * BLOCK, BLOCK), BLOCK)]

    def up_hops(j):
        return 4 - j % 2

    def down_hops(j):
        return 3 + j % 2

    def pass_on(j, s):
        if s < up_hops(j):
            block = piece((z + ZS - s) % ZS, j)
            start(block, block, up_send.at[s, j], up_recv.at[s, j], at((z + 1) % ZS, e), tp)
        if s < down_hops(j):
            block = piece((z + s) % ZS, j)
            start(block, block, dn_send.at[s, j], dn_recv.at[s, j], at((z + ZS - 1) % ZS, e), tp)

    def begin(group):
        for k in range(1, PLANE):
            rows = pl.ds(pl.multiple_of(z * BLOCK + partner(k) * ROWS, ROWS), ROWS)
            arrived(wbuf.at[pl.ds(2 * group, 2), rows], wy_recv.at[group, k])
        pass_on(2 * group, 0)
        pass_on(2 * group + 1, 0)

    def forward(j, s):
        if s < up_hops(j):
            arrived(piece((z + 2 * ZS - 1 - s) % ZS, j), up_recv.at[s, j])
        if s < down_hops(j):
            arrived(piece((z + 1 + s) % ZS, j), dn_recv.at[s, j])
        pass_on(j, s + 1)

    for k in range(4, 8):
        loads[k].wait()
    for g in range(GROUPS):
        cols = slice(g * LANES, (g + 1) * LANES)
        places = pl.ds(g, MODES, stride=GROUPS)
        decay[places, :] = jnp.exp(-rate[:, cols])
        late[places, :] = jnp.exp(rate[:, cols] * (-float(TOK - HEAD)))
        power[places, :] = rate[:, cols]
        gain[places, :] = resid[:, cols]

    row_id = lax.broadcasted_iota(jnp.int32, (TOK, LANES), 0)

    def featured_part(p, cols):
        now = proj[p, :, cols].astype(jnp.float32)
        taps = filt[p, :, cols]
        one = jnp.where(row_id >= 1, pltpu.roll(now, 1, 0), 0.0)
        two = jnp.where(row_id >= 2, pltpu.roll(now, 2, 0), 0.0)
        return taps[0:1, :] * now + taps[1:2, :] * one + taps[2:3, :] * two

    def featurize_gates(g, carry_in):
        cols = pl.ds(pl.multiple_of(g * LANES, LANES), LANES)
        gates[pl.ds(pl.multiple_of(g * TOK, TOK), TOK), :] = (
            (featured_part(1, cols) * featured_part(2, cols)).astype(jnp.bfloat16)
        ).astype(jnp.float32)
        return carry_in

    def featurize_query(g, carry_in):
        cols = pl.ds(pl.multiple_of(g * LANES, LANES), LANES)
        query[:, cols] = featured_part(0, cols)
        return carry_in

    lax.fori_loop(0, GROUPS, featurize_gates, 0)

    def token(ref, t):
        return ref[pl.ds(t, GROUPS, stride=TOK), :]

    def mode(ref, n):
        return ref[n * GROUPS : (n + 1) * GROUPS, :]

    def summed(terms):
        while len(terms) > 1:
            terms = [
                terms[i] + terms[i + 1] if i + 1 < len(terms) else terms[i]
                for i in range(0, len(terms), 2)
            ]
        return terms[0]

    zero = tuple(jnp.zeros((GROUPS, LANES), jnp.float32) for _ in range(MODES))

    def local_filter(step, held):
        for u in range(HEAD):
            t = step * HEAD + u
            g_now = token(gates, t)
            held = tuple(mode(decay, n) * held[n] + g_now for n in range(MODES))
            terms = [mode(gain, n) * held[n] for n in range(MODES)]
            conv[pl.ds(t, GROUPS, stride=TOK), :] = summed(terms + [skip[...] * g_now])
        return held

    steps = TOK // HEAD
    tail = lax.fori_loop(1, steps // 2, local_filter, zero)
    tail = lax.fori_loop(steps // 2, steps, local_filter, tail)
    for n in range(MODES):
        state[n * GROUPS : (n + 1) * GROUPS, :] = tail[n]

    @pl.when(ctx > 0)
    def _():
        remote(halo_in, halo_in, halo_send.at[0], halo_recv.at[0], ctx - 1, tp).wait_recv()

    edge_id = lax.broadcasted_iota(jnp.int32, (HEAD, CHAN), 0)
    featured = []
    for p in range(3):
        now = proj[p, 0:16, :].astype(jnp.float32)[0:HEAD, :]
        before2 = halo_in[2 * p : 2 * p + 1, :]
        before1 = halo_in[2 * p + 1 : 2 * p + 2, :]
        one = jnp.where(edge_id >= 1, pltpu.roll(now, 1, 0), before1)
        two = jnp.where(
            edge_id >= 2, pltpu.roll(now, 2, 0), jnp.where(edge_id == 0, before2, before1)
        )
        taps = filt[p]
        featured.append(taps[0:1, :] * now + taps[1:2, :] * one + taps[2:3, :] * two)
    first = (featured[1] * featured[2]).astype(jnp.bfloat16).astype(jnp.float32)
    for g in range(GROUPS):
        gates[g * TOK : g * TOK + HEAD, :] = first[:, g * LANES : (g + 1) * LANES]
    opening = lax.fori_loop(0, 1, local_filter, zero)
    for n in range(MODES):
        rows = slice(n * GROUPS, (n + 1) * GROUPS)
        head[rows, :] = opening[n]
        state[rows, :] = state[rows, :] + late[rows, :] * opening[n]

    own_modes = pl.ds(pl.multiple_of(e * 16, 16), 16)
    for k in range(1, PLANE):
        ee = (e + k) % PLANE
        start(
            state.at[pl.ds(pl.multiple_of(ee * 16, 16), 16)],
            stage1.at[e],
            s1_send.at[k],
            s1_recv.at[k],
            at(z, ee),
            tp,
        )
    stage1[e] = state[own_modes, :]

    begin(0)
    begin(1)
    lax.fori_loop(0, GROUPS, featurize_query, 0)
    query[0:HEAD, :] = featured[0]
    forward(0, 0)
    forward(1, 0)

    for k in range(1, PLANE):
        arrived(stage1.at[(e + PLANE - k) % PLANE], s1_recv.at[k])
    rates = power[own_modes, :]
    over_device = jnp.exp(rates * (-float(TOK)))
    over_plane = jnp.exp(rates * (-float(TOK * PLANE)))
    running = stage1[0]
    for k in range(1, PLANE):
        running = over_device * running + stage1[k]
    total[...] = running
    for k in range(1, ZS):
        start(total, stage2.at[z], s2_send.at[k], s2_recv.at[k], at((z + k) % ZS, e), tp)
    stage2[z] = running

    forward(2, 0)
    forward(3, 0)
    forward(0, 1)
    forward(1, 1)

    for k in range(1, ZS):
        arrived(stage2.at[(z + ZS - k) % ZS], s2_recv.at[k])
    running = jnp.zeros((16, LANES), jnp.float32)
    for k in range(ZS - 1):
        running = jnp.where(k < z, over_plane * running + stage2[k], running)
    for k in range(PLANE):
        carries[k] = running
        if k < PLANE - 1:
            running = over_device * running + stage1[k]
    for k in range(1, PLANE):
        ee = (e + k) % PLANE
        start(carries.at[ee], carry.at[own_modes], s3_send.at[k], s3_recv.at[k], at(z, ee), tp)
    carry[own_modes, :] = carries[e]

    forward(2, 1)
    forward(3, 1)
    forward(0, 2)
    forward(1, 2)

    for k in range(1, PLANE):
        ee = (e + PLANE - k) % PLANE
        arrived(carry.at[pl.ds(pl.multiple_of(ee * 16, 16), 16)], s3_recv.at[k])

    def add_carry(step, held):
        for u in range(HEAD):
            t = step * HEAD + u
            held = tuple(mode(decay, n) * held[n] for n in range(MODES))
            conv[pl.ds(t, GROUPS, stride=TOK), :] = summed(list(held) + [token(conv, t)])
        return held

    across = member(1 - par, c)
    sibling = member(par, 1 - c)

    def direct(part):
        first, count = PARTS[part]
        return pl.ds(2 * TOK + 2 * first, count)

    def indirect(part):
        first, count = PARTS[part]
        return pl.ds(2 * TOK + 2 * first + count, count)

    def mix(part):
        first, count = PARTS[part]
        rows = slice(first, first + count)

        def mix_group(g, carry_in):
            cols = pl.ds(pl.multiple_of(g * LANES, LANES), LANES)
            places = pl.ds(pl.multiple_of(g * TOK + first, count), count)
            filtered = conv[places, :].astype(jnp.bfloat16).astype(jnp.float32)
            mixed[rows, cols] = (query[rows, cols] * filtered).astype(jnp.bfloat16)
            return carry_in

        lax.fori_loop(0, GROUPS, mix_group, 0)
        mine = mixed.at[pl.ds(first, count)]
        there = mixed.at[direct(part)]
        start(mine, there, mix_send.at[part, 0], mix_recv.at[part, 0], across, tp)
        there = mixed.at[pl.ds(TOK + first, count)]
        start(mine, there, mix_send.at[part, 1], mix_recv.at[part, 1], sibling, tp)

    held = tuple(mode(gain, n) * mode(carry, n) for n in range(MODES))
    held = lax.fori_loop(0, 1, add_carry, held)
    held = tuple(held[n] + mode(gain, n) * mode(head, n) for n in range(MODES))
    held = lax.fori_loop(1, steps // 2, add_carry, held)
    mix(0)
    forward(2, 2)
    forward(3, 2)
    held = lax.fori_loop(steps // 2, steps * 3 // 4, add_carry, held)
    mix(1)
    lax.fori_loop(steps * 3 // 4, steps, add_carry, held)
    mix(2)
    forward(0, 3)

    chunks = [(0, TOK), (TOK, TOK)] + [(2 * TOK + 2 * first, 2 * count) for first, count in PARTS]

    def product(m, d):
        first, count = chunks[m]
        return jnp.dot(
            mixed[first : first + count, :],
            wbuf[ORDER.index(d)],
            preferred_element_type=jnp.float32,
        )

    right = ((x + 1) % XS) * 2 + h
    left = ((x + XS - 1) % XS) * 2 + h

    def spans(m):
        first, count = chunks[m]
        half = count // 2
        return pl.ds(first, count), pl.ds(first, half), pl.ds(first + half, half), half

    def far_terms(m):
        every, upper, lower, _ = spans(m)
        far_out[every, :] = product(m, 2).astype(jnp.bfloat16)
        into = far_in.at[upper]
        start(far_out.at[upper], into, x_send.at[m, 0], x_recv.at[m, 0], ctx, right)
        into = far_in.at[lower]
        start(far_out.at[lower], into, x_send.at[m, 1], x_recv.at[m, 1], ctx, left)

    def near_terms(m):
        every, upper, lower, half = spans(m)
        term = product(m, 1)
        up_out[lower, :] = term[half:].astype(jnp.bfloat16)
        arrived(far_in.at[upper], x_recv.at[m, 0])
        up_out[upper, :] = (term[:half] + far_in[upper, :].astype(jnp.float32)).astype(jnp.bfloat16)
        start(up_out.at[every], up_in.at[every], x_send.at[m, 2], x_recv.at[m, 2], ctx, right)
        term = product(m, 3)
        down_out[upper, :] = term[:half].astype(jnp.bfloat16)
        arrived(far_in.at[lower], x_recv.at[m, 1])
        down_out[lower, :] = (term[half:] + far_in[lower, :].astype(jnp.float32)).astype(
            jnp.bfloat16
        )
        start(down_out.at[every], down_in.at[every], x_send.at[m, 3], x_recv.at[m, 3], ctx, left)

    last = []
    my_columns = pl.ds(pl.multiple_of(c * PIECE, PIECE), PIECE)
    stay = pltpu.make_async_copy(half_out.at[pl.ds(0, TOK)], out.at[h, :, my_columns], stay_sem)

    def own_terms(m):
        every, upper, lower, half = spans(m)
        term = product(m, 0)
        arrived(up_in.at[every], x_recv.at[m, 2])
        arrived(down_in.at[every], x_recv.at[m, 3])
        both = up_in[every, :].astype(jnp.float32) + down_in[every, :].astype(jnp.float32)
        half_out[every, :] = (term + both).astype(jnp.bfloat16)
        if m < 2:
            moves = [(member(par, (c + m) % 2), every, pl.ds(0, TOK), 3)]
        else:
            place = pl.ds(*PARTS[m - 2])
            moves = [
                (member(1 - par, c), upper, place, m - 2),
                (member(1 - par, 1 - c), lower, place, m - 2),
            ]
        for k, (to, rows, place, slot) in enumerate(moves):
            copy = remote(
                half_out.at[rows],
                out.at[h, place, my_columns],
                h_send.at[m, k],
                h_recv.at[h, c, slot],
                to,
                x * 2 + par,
            )
            if m == 0:

                @pl.when(h == par)
                def _():
                    stay.start()

                @pl.when(h != par)
                def _():
                    copy.start()
            else:
                copy.start()
            last.append((copy, m == 0))

    def from_across(part):
        rows = direct(part)
        arrived(mixed.at[rows], mix_recv.at[part, 0])
        there = mixed.at[indirect(part)]
        start(mixed.at[rows], there, mix_send.at[part, 2], mix_recv.at[part, 2], sibling, tp)

    def from_sibling(part):
        arrived(mixed.at[indirect(part)], mix_recv.at[part, 2])

    far_terms(0)
    for part, (first, count) in enumerate(PARTS):
        arrived(mixed.at[pl.ds(TOK + first, count)], mix_recv.at[part, 1])
    far_terms(1)
    forward(1, 3)
    forward(2, 3)
    near_terms(0)
    from_across(0)
    near_terms(1)
    from_sibling(0)
    far_terms(2)
    from_across(1)
    forward(3, 3)
    own_terms(0)
    from_sibling(1)
    far_terms(3)
    from_across(2)
    near_terms(2)
    from_sibling(2)
    far_terms(4)
    own_terms(1)
    near_terms(3)
    near_terms(4)
    own_terms(2)
    own_terms(3)
    own_terms(4)

    for k in range(4):
        hs, cs = (h + k // 2) % 2, (c + k) % 2
        columns = pl.ds(pl.multiple_of(cs * PIECE, PIECE), PIECE)
        if k > 0:

            @pl.when(par == h)
            def _(hs=hs, cs=cs, columns=columns):
                arrived(out.at[hs, :, columns], h_recv.at[hs, cs, 3])

        @pl.when(par != h)
        def _(hs=hs, cs=cs, columns=columns):
            for part, (first, count) in enumerate(PARTS):
                arrived(out.at[hs, pl.ds(first, count), columns], h_recv.at[hs, cs, part])

    @pl.when(h == par)
    def _():
        stay.wait()

    @pl.when(ctx < ZS * PLANE - 1)
    def _():
        halo_copy.wait_send()

    for copy in sent:
        copy.wait_send()
    for copy, may_stay in last:
        if may_stay:

            @pl.when(h != par)
            def _():
                copy.wait_send()
        else:
            copy.wait_send()


def on_device(projected, short_filter, decay_rate, residue, skip_gain, out_weight):
    f32, bf16 = jnp.float32, jnp.bfloat16
    dma = pltpu.SemaphoreType.DMA
    table = pltpu.VMEM((MODES * GROUPS, LANES), f32)
    sums = pltpu.VMEM((4 * TOK, PIECE), bf16)
    scratch = [
        pltpu.VMEM((3, TOK, CHAN), bf16),
        pltpu.VMEM((3, 3, CHAN), f32),
        pltpu.VMEM((MODES, CHAN), f32),
        pltpu.VMEM((MODES, CHAN), f32),
        pltpu.VMEM((GROUPS, LANES), f32),
        pltpu.VMEM((ROWS, 4096), bf16),
        pltpu.VMEM((4, XS, ROWS, PIECE), bf16),
        pltpu.VMEM((XS, CHAN, PIECE), bf16),
        pltpu.VMEM((8, CHAN), f32),
        pltpu.VMEM((8, CHAN), f32),
        pltpu.VMEM((GROUPS * TOK, LANES), f32),
        pltpu.VMEM((TOK, CHAN), f32),
        pltpu.VMEM((GROUPS * TOK, LANES), f32),
        table,
        table,
        table,
        table,
        table,
        table,
        pltpu.VMEM((PLANE, 16, LANES), f32),
        pltpu.VMEM((16, LANES), f32),
        pltpu.VMEM((ZS, 16, LANES), f32),
        pltpu.VMEM((PLANE, 16, LANES), f32),
        table,
        pltpu.VMEM((4 * TOK, CHAN), bf16),
        sums,
        sums,
        sums,
        sums,
        sums,
        sums,
        sums,
        dma,
        dma((8,)),
        dma((1,)),
        dma((1,)),
        dma((2, PLANE)),
        dma((2, PLANE)),
        dma((4, 4)),
        dma((4, 4)),
        dma((4, 4)),
        dma((4, 4)),
        dma((PLANE,)),
        dma((PLANE,)),
        dma((ZS,)),
        dma((ZS,)),
        dma((PLANE,)),
        dma((PLANE,)),
        dma((3, 3)),
        dma((3, 3)),
        dma((5, 4)),
        dma((5, 4)),
        dma((5, 2)),
        dma((2, 2, 4)),
    ]
    halves = pl.pallas_call(
        block_kernel,
        out_shape=jax.ShapeDtypeStruct((2, TOK, 2 * PIECE), bf16),
        in_specs=[pl.BlockSpec(memory_space=pltpu.HBM)] * 6,
        out_specs=pl.BlockSpec(memory_space=pltpu.HBM),
        scratch_shapes=scratch,
        compiler_params=pltpu.CompilerParams(
            collective_id=0, has_side_effects=True, vmem_limit_bytes=61 * 1024 * 1024
        ),
    )(
        projected,
        short_filter,
        decay_rate.T,
        residue.T,
        skip_gain.reshape(GROUPS, LANES),
        out_weight,
    )
    return (halves[0].astype(f32) + halves[1].astype(f32)).astype(bf16)


def solution(mesh):
    in_specs = (
        P(None, "ctx", "tp"),
        P(None, None, "tp"),
        P("tp", None),
        P("tp", None),
        P("tp"),
        P(("tp", "ctx"), None),
    )
    out_specs = P("ctx", "tp")
    return jax.shard_map(
        on_device, mesh=mesh, in_specs=in_specs, out_specs=out_specs, check_vma=False
    )
```

```python
import jax
import jax.numpy as jnp
from jax import lax
from jax.experimental import pallas as pl
from jax.experimental.pallas import tpu as pltpu
from jax.sharding import PartitionSpec as P

ZS = 8
PLANE = 8
XS = 4
TOK = 256
CHAN = 1024
LANES = 128
GROUPS = CHAN // LANES
MODES = 16
ROWS = 16
BLOCK = PLANE * ROWS
ORDER = (2, 1, 3, 0)
PIECE = 256
HEAD = 8
PARTS = ((0, 128), (128, 64), (192, 64))


def block_kernel(
    proj_hbm,
    filt_hbm,
    rate_hbm,
    resid_hbm,
    skip_hbm,
    weight_hbm,
    out,
    proj,
    filt,
    rate,
    resid,
    skip,
    weight,
    wq,
    wbuf,
    halo_out,
    halo_in,
    gates,
    query,
    conv,
    decay,
    gain,
    power,
    late,
    head,
    state,
    stage1,
    total,
    stage2,
    carries,
    carry,
    mixed,
    far_out,
    up_out,
    down_out,
    far_in,
    up_in,
    down_in,
    half_out,
    stay_sem,
    load_sem,
    halo_send,
    halo_recv,
    wy_send,
    wy_recv,
    up_send,
    up_recv,
    dn_send,
    dn_recv,
    s1_send,
    s1_recv,
    s2_send,
    s2_recv,
    s3_send,
    s3_recv,
    mix_send,
    mix_recv,
    x_send,
    x_recv,
    h_send,
    h_recv,
):
    ctx = lax.axis_index("ctx")
    tp = lax.axis_index("tp")
    z = ctx // PLANE
    e = ctx % PLANE
    c = e % 2
    par = (e // 2) % 2
    quad = e // 4
    x = tp // 2
    h = tp % 2

    def at(zz, ee):
        return zz * PLANE + ee

    def partner(k):
        return ((e // 4 + k // 4) % 2) * 4 + ((e // 2 + k // 2) % 2) * 2 + (e + k) % 2

    def member(pp, cc):
        return z * PLANE + quad * 4 + pp * 2 + cc

    def remote(src, dst, send, recv, to_ctx, to_tp):
        return pltpu.make_async_remote_copy(
            src_ref=src,
            dst_ref=dst,
            send_sem=send,
            recv_sem=recv,
            device_id={"ctx": to_ctx, "tp": to_tp},
            device_id_type=pl.DeviceIdType.MESH,
        )

    sent = []

    def start(*args):
        copy = remote(*args)
        copy.start()
        sent.append(copy)

    def arrived(dst, recv):
        remote(dst, dst, recv, recv, at((z + 1) % ZS, e), tp).wait_recv()

    barrier = pltpu.get_barrier_semaphore()

    def greet(to_ctx, to_tp):
        pl.semaphore_signal(
            barrier,
            inc=1,
            device_id={"ctx": to_ctx, "tp": to_tp},
            device_id_type=pl.DeviceIdType.MESH,
        )

    for k in range(1, PLANE):
        greet(at(z, (e + k) % PLANE), tp)
    for k in range(1, ZS):
        greet(at((z + k) % ZS, e), tp)
    for k in (1, XS - 1):
        greet(ctx, ((x + k) % XS) * 2 + h)
    for pp in range(2):
        for cc in range(2):
            greet(member(pp, cc), x * 2 + (1 - h))
    to_next = jnp.logical_and(e == PLANE - 1, z < ZS - 1)
    to_prev = jnp.logical_and(e == 0, z > 0)

    @pl.when(to_next)
    def _():
        greet(ctx + 1, tp)

    @pl.when(to_prev)
    def _():
        greet(ctx - 1, tp)

    loads = [
        pltpu.make_async_copy(src, dst, load_sem.at[k])
        for k, (src, dst) in enumerate(
            [
                (weight_hbm, weight),
                (proj_hbm.at[1], proj.at[1]),
                (proj_hbm.at[2], proj.at[2]),
                (proj_hbm.at[0], proj.at[0]),
                (rate_hbm, rate),
                (filt_hbm, filt),
                (resid_hbm, resid),
                (skip_hbm, skip),
            ]
        )
    ]
    for copy in loads:
        copy.start()

    loads[0].wait()
    for q in range(4):
        pp, cc = q // 2, q % 2
        for j in range(XS):
            for hh in range(2):
                col = (x + ORDER[j]) % XS * 1024 + hh * 512 + (pp * 2 + cc) * LANES
                wq[q, j, :, hh * LANES : (hh + 1) * LANES] = weight[
                    :, pl.ds(pl.multiple_of(col, LANES), LANES)
                ]
    for k in range(1, 4):
        loads[k].wait()
    for p in range(3):
        rim = proj[p, TOK - 16 : TOK, :].astype(jnp.float32)
        halo_out[2 * p : 2 * p + 2, :] = rim[14:16, :]
    halo_out[6:8, :] = jnp.zeros((2, CHAN), jnp.float32)

    @pl.when(ctx == 0)
    def _():
        halo_in[...] = jnp.zeros_like(halo_in)

    beyond = jnp.logical_or(to_next, to_prev).astype(jnp.int32)
    pl.semaphore_wait(barrier, 7 + 7 + 2 + 4 + beyond)

    halo_copy = remote(halo_out, halo_in, halo_send.at[0], halo_recv.at[0], ctx + 1, tp)

    @pl.when(ctx < ZS * PLANE - 1)
    def _():
        halo_copy.start()

    my_rows = pl.ds(pl.multiple_of(z * BLOCK + e * ROWS, ROWS), ROWS)
    groups = (pl.ds(0, 3), pl.ds(3, 1))

    def plane_shares(group):
        js = groups[group]
        for k in range(1, PLANE):
            ee = partner(k)
            share = ((ee // 2) % 2) * 2 + ee % 2
            start(
                wq.at[share, js],
                wbuf.at[js, my_rows],
                wy_send.at[group, k],
                wy_recv.at[group, k],
                at(z, ee),
                tp,
            )

    plane_shares(0)
    wbuf[:, my_rows, :] = wq[par * 2 + c]

    def piece(zz, j):
        return wbuf.at[j, pl.ds(pl.multiple_of(zz * BLOCK, BLOCK), BLOCK)]

    def up_hops(j):
        return 4 - j % 2

    def down_hops(j):
        return 3 + j % 2

    def pass_on(j, s):
        if s < up_hops(j):
            block = piece((z + ZS - s) % ZS, j)
            start(block, block, up_send.at[s, j], up_recv.at[s, j], at((z + 1) % ZS, e), tp)
        if s < down_hops(j):
            block = piece((z + s) % ZS, j)
            start(block, block, dn_send.at[s, j], dn_recv.at[s, j], at((z + ZS - 1) % ZS, e), tp)

    def begin(group):
        for k in range(1, PLANE):
            rows = pl.ds(pl.multiple_of(z * BLOCK + partner(k) * ROWS, ROWS), ROWS)
            arrived(wbuf.at[groups[group], rows], wy_recv.at[group, k])
        for j in (range(3), range(3, 4))[group]:
            pass_on(j, 0)

    def forward(j, s):
        if s < up_hops(j):
            arrived(piece((z + 2 * ZS - 1 - s) % ZS, j), up_recv.at[s, j])
        if s < down_hops(j):
            arrived(piece((z + 1 + s) % ZS, j), dn_recv.at[s, j])
        pass_on(j, s + 1)

    for k in range(4, 8):
        loads[k].wait()
    for g in range(GROUPS):
        cols = slice(g * LANES, (g + 1) * LANES)
        places = pl.ds(g, MODES, stride=GROUPS)
        decay[places, :] = jnp.exp(-rate[:, cols])
        late[places, :] = jnp.exp(rate[:, cols] * (-float(TOK - HEAD)))
        power[places, :] = rate[:, cols]
        gain[places, :] = resid[:, cols]

    row_id = lax.broadcasted_iota(jnp.int32, (TOK, LANES), 0)

    def featured_part(p, cols):
        now = proj[p, :, cols].astype(jnp.float32)
        taps = filt[p, :, cols]
        one = jnp.where(row_id >= 1, pltpu.roll(now, 1, 0), 0.0)
        two = jnp.where(row_id >= 2, pltpu.roll(now, 2, 0), 0.0)
        return taps[0:1, :] * now + taps[1:2, :] * one + taps[2:3, :] * two

    def featurize_gates(g, carry_in):
        cols = pl.ds(pl.multiple_of(g * LANES, LANES), LANES)
        gates[pl.ds(pl.multiple_of(g * TOK, TOK), TOK), :] = (
            (featured_part(1, cols) * featured_part(2, cols)).astype(jnp.bfloat16)
        ).astype(jnp.float32)
        return carry_in

    def featurize_query(g, carry_in):
        cols = pl.ds(pl.multiple_of(g * LANES, LANES), LANES)
        query[:, cols] = featured_part(0, cols)
        return carry_in

    lax.fori_loop(0, GROUPS, featurize_gates, 0)

    def token(ref, t):
        return ref[pl.ds(t, GROUPS, stride=TOK), :]

    def mode(ref, n):
        return ref[n * GROUPS : (n + 1) * GROUPS, :]

    def summed(terms):
        while len(terms) > 1:
            terms = [
                terms[i] + terms[i + 1] if i + 1 < len(terms) else terms[i]
                for i in range(0, len(terms), 2)
            ]
        return terms[0]

    zero = tuple(jnp.zeros((GROUPS, LANES), jnp.float32) for _ in range(MODES))

    def local_filter(step, held):
        for u in range(HEAD):
            t = step * HEAD + u
            g_now = token(gates, t)
            held = tuple(mode(decay, n) * held[n] + g_now for n in range(MODES))
            terms = [mode(gain, n) * held[n] for n in range(MODES)]
            conv[pl.ds(t, GROUPS, stride=TOK), :] = summed(terms + [skip[...] * g_now])
        return held

    steps = TOK // HEAD
    tail = lax.fori_loop(1, steps // 2, local_filter, zero)
    tail = lax.fori_loop(steps // 2, steps, local_filter, tail)
    for n in range(MODES):
        state[n * GROUPS : (n + 1) * GROUPS, :] = tail[n]

    @pl.when(ctx > 0)
    def _():
        remote(halo_in, halo_in, halo_send.at[0], halo_recv.at[0], ctx - 1, tp).wait_recv()

    edge_id = lax.broadcasted_iota(jnp.int32, (HEAD, CHAN), 0)
    featured = []
    for p in range(3):
        now = proj[p, 0:16, :].astype(jnp.float32)[0:HEAD, :]
        before2 = halo_in[2 * p : 2 * p + 1, :]
        before1 = halo_in[2 * p + 1 : 2 * p + 2, :]
        one = jnp.where(edge_id >= 1, pltpu.roll(now, 1, 0), before1)
        two = jnp.where(
            edge_id >= 2, pltpu.roll(now, 2, 0), jnp.where(edge_id == 0, before2, before1)
        )
        taps = filt[p]
        featured.append(taps[0:1, :] * now + taps[1:2, :] * one + taps[2:3, :] * two)
    first = (featured[1] * featured[2]).astype(jnp.bfloat16).astype(jnp.float32)
    for g in range(GROUPS):
        gates[g * TOK : g * TOK + HEAD, :] = first[:, g * LANES : (g + 1) * LANES]
    opening = lax.fori_loop(0, 1, local_filter, zero)
    for n in range(MODES):
        rows = slice(n * GROUPS, (n + 1) * GROUPS)
        head[rows, :] = opening[n]
        state[rows, :] = state[rows, :] + late[rows, :] * opening[n]

    own_modes = pl.ds(pl.multiple_of(e * 16, 16), 16)
    for k in range(1, PLANE):
        ee = (e + k) % PLANE
        start(
            state.at[pl.ds(pl.multiple_of(ee * 16, 16), 16)],
            stage1.at[e],
            s1_send.at[k],
            s1_recv.at[k],
            at(z, ee),
            tp,
        )
    stage1[e] = state[own_modes, :]

    lax.fori_loop(0, GROUPS, featurize_query, 0)
    query[0:HEAD, :] = featured[0]
    begin(0)
    plane_shares(1)
    forward(0, 0)

    for k in range(1, PLANE):
        arrived(stage1.at[(e + PLANE - k) % PLANE], s1_recv.at[k])
    rates = power[own_modes, :]
    over_device = jnp.exp(rates * (-float(TOK)))
    over_plane = jnp.exp(rates * (-float(TOK * PLANE)))
    running = stage1[0]
    for k in range(1, PLANE):
        running = over_device * running + stage1[k]
    total[...] = running
    for k in range(1, ZS):
        start(total, stage2.at[z], s2_send.at[k], s2_recv.at[k], at((z + k) % ZS, e), tp)
    stage2[z] = running

    forward(1, 0)
    forward(2, 0)
    forward(0, 1)

    for k in range(1, ZS):
        arrived(stage2.at[(z + ZS - k) % ZS], s2_recv.at[k])
    running = jnp.zeros((16, LANES), jnp.float32)
    for k in range(ZS - 1):
        running = jnp.where(k < z, over_plane * running + stage2[k], running)
    for k in range(PLANE):
        carries[k] = running
        if k < PLANE - 1:
            running = over_device * running + stage1[k]
    for k in range(1, PLANE):
        ee = (e + k) % PLANE
        start(carries.at[ee], carry.at[own_modes], s3_send.at[k], s3_recv.at[k], at(z, ee), tp)
    carry[own_modes, :] = carries[e]

    forward(1, 1)
    forward(2, 1)
    forward(0, 2)
    begin(1)

    for k in range(1, PLANE):
        ee = (e + PLANE - k) % PLANE
        arrived(carry.at[pl.ds(pl.multiple_of(ee * 16, 16), 16)], s3_recv.at[k])

    def add_carry(step, held):
        for u in range(HEAD):
            t = step * HEAD + u
            held = tuple(mode(decay, n) * held[n] for n in range(MODES))
            conv[pl.ds(t, GROUPS, stride=TOK), :] = summed(list(held) + [token(conv, t)])
        return held

    across = member(1 - par, c)
    sibling = member(par, 1 - c)

    def direct(part):
        first, count = PARTS[part]
        return pl.ds(2 * TOK + 2 * first, count)

    def indirect(part):
        first, count = PARTS[part]
        return pl.ds(2 * TOK + 2 * first + count, count)

    def mix(part):
        first, count = PARTS[part]
        rows = slice(first, first + count)

        def mix_group(g, carry_in):
            cols = pl.ds(pl.multiple_of(g * LANES, LANES), LANES)
            places = pl.ds(pl.multiple_of(g * TOK + first, count), count)
            filtered = conv[places, :].astype(jnp.bfloat16).astype(jnp.float32)
            mixed[rows, cols] = (query[rows, cols] * filtered).astype(jnp.bfloat16)
            return carry_in

        lax.fori_loop(0, GROUPS, mix_group, 0)
        mine = mixed.at[pl.ds(first, count)]
        there = mixed.at[direct(part)]
        start(mine, there, mix_send.at[part, 0], mix_recv.at[part, 0], across, tp)
        there = mixed.at[pl.ds(TOK + first, count)]
        start(mine, there, mix_send.at[part, 1], mix_recv.at[part, 1], sibling, tp)

    held = tuple(mode(gain, n) * mode(carry, n) for n in range(MODES))
    held = lax.fori_loop(0, 1, add_carry, held)
    held = tuple(held[n] + mode(gain, n) * mode(head, n) for n in range(MODES))
    held = lax.fori_loop(1, steps // 2, add_carry, held)
    mix(0)
    forward(1, 2)
    forward(2, 2)
    held = lax.fori_loop(steps // 2, steps * 3 // 4, add_carry, held)
    mix(1)
    lax.fori_loop(steps * 3 // 4, steps, add_carry, held)
    mix(2)
    forward(0, 3)

    chunks = [(0, TOK), (TOK, TOK)] + [(2 * TOK + 2 * first, 2 * count) for first, count in PARTS]

    def product(m, d):
        first, count = chunks[m]
        return jnp.dot(
            mixed[first : first + count, :],
            wbuf[ORDER.index(d)],
            preferred_element_type=jnp.float32,
        )

    right = ((x + 1) % XS) * 2 + h
    left = ((x + XS - 1) % XS) * 2 + h

    def spans(m):
        first, count = chunks[m]
        half = count // 2
        return pl.ds(first, count), pl.ds(first, half), pl.ds(first + half, half), half

    def far_terms(m):
        every, upper, lower, _ = spans(m)
        far_out[every, :] = product(m, 2).astype(jnp.bfloat16)
        into = far_in.at[upper]
        start(far_out.at[upper], into, x_send.at[m, 0], x_recv.at[m, 0], ctx, right)
        into = far_in.at[lower]
        start(far_out.at[lower], into, x_send.at[m, 1], x_recv.at[m, 1], ctx, left)

    def near_terms(m):
        every, upper, lower, half = spans(m)
        term = product(m, 1)
        up_out[lower, :] = term[half:].astype(jnp.bfloat16)
        arrived(far_in.at[upper], x_recv.at[m, 0])
        up_out[upper, :] = (term[:half] + far_in[upper, :].astype(jnp.float32)).astype(jnp.bfloat16)
        start(up_out.at[every], up_in.at[every], x_send.at[m, 2], x_recv.at[m, 2], ctx, right)
        term = product(m, 3)
        down_out[upper, :] = term[:half].astype(jnp.bfloat16)
        arrived(far_in.at[lower], x_recv.at[m, 1])
        down_out[lower, :] = (term[half:] + far_in[lower, :].astype(jnp.float32)).astype(
            jnp.bfloat16
        )
        start(down_out.at[every], down_in.at[every], x_send.at[m, 3], x_recv.at[m, 3], ctx, left)

    last = []
    my_columns = pl.ds(pl.multiple_of((par * 2 + c) * LANES, LANES), LANES)

    def of_half(hh):
        return pl.ds(pl.multiple_of(hh * LANES, LANES), LANES)

    stay = pltpu.make_async_copy(
        half_out.at[pl.ds(0, TOK), of_half(h)], out.at[h, :, my_columns], stay_sem
    )

    def own_terms(m):
        every, upper, lower, half = spans(m)
        term = product(m, 0)
        arrived(up_in.at[every], x_recv.at[m, 2])
        arrived(down_in.at[every], x_recv.at[m, 3])
        both = up_in[every, :].astype(jnp.float32) + down_in[every, :].astype(jnp.float32)
        half_out[every, :] = (term + both).astype(jnp.bfloat16)
        if m < 2:
            moves = [(member(par, (c + m) % 2), every, pl.ds(0, TOK), 3)]
        else:
            place = pl.ds(*PARTS[m - 2])
            moves = [
                (member(1 - par, c), upper, place, m - 2),
                (member(1 - par, 1 - c), lower, place, m - 2),
            ]
        for a in (1, 0):
            hh = (h + a) % 2
            for k, (to, rows, place, slot) in enumerate(moves):
                if m == 0 and a == 0:
                    stay.start()
                    continue
                copy = remote(
                    half_out.at[rows, of_half(hh)],
                    out.at[h, place, my_columns],
                    h_send.at[m, a, k],
                    h_recv.at[h, par * 2 + c, slot],
                    to,
                    x * 2 + hh,
                )
                copy.start()
                last.append(copy)

    def from_across(part):
        rows = direct(part)
        arrived(mixed.at[rows], mix_recv.at[part, 0])
        there = mixed.at[indirect(part)]
        start(mixed.at[rows], there, mix_send.at[part, 2], mix_recv.at[part, 2], sibling, tp)

    def from_sibling(part):
        arrived(mixed.at[indirect(part)], mix_recv.at[part, 2])

    far_terms(0)
    for part, (first, count) in enumerate(PARTS):
        arrived(mixed.at[pl.ds(TOK + first, count)], mix_recv.at[part, 1])
    far_terms(1)
    forward(3, 0)
    forward(1, 3)
    forward(2, 3)
    near_terms(0)
    forward(3, 1)
    from_across(0)
    near_terms(1)
    forward(3, 2)
    from_sibling(0)
    far_terms(2)
    from_across(1)
    forward(3, 3)
    own_terms(0)
    from_sibling(1)
    far_terms(3)
    from_across(2)
    near_terms(2)
    from_sibling(2)
    far_terms(4)
    own_terms(1)
    near_terms(3)
    near_terms(4)
    own_terms(2)
    own_terms(3)
    own_terms(4)

    for k in range(8):
        hs, ps, cs = (h + k // 4) % 2, (par + k // 2) % 2, (c + k) % 2
        columns = pl.ds(pl.multiple_of((ps * 2 + cs) * LANES, LANES), LANES)
        if k == 0:
            stay.wait()
        elif k // 2 % 2 == 0:
            arrived(out.at[hs, :, columns], h_recv.at[hs, ps * 2 + cs, 3])
        else:
            for part, (first, count) in enumerate(PARTS):
                place = out.at[hs, pl.ds(first, count), columns]
                arrived(place, h_recv.at[hs, ps * 2 + cs, part])

    @pl.when(ctx < ZS * PLANE - 1)
    def _():
        halo_copy.wait_send()

    for copy in sent:
        copy.wait_send()
    for copy in last:
        copy.wait_send()


def on_device(projected, short_filter, decay_rate, residue, skip_gain, out_weight):
    f32, bf16 = jnp.float32, jnp.bfloat16
    dma = pltpu.SemaphoreType.DMA
    table = pltpu.VMEM((MODES * GROUPS, LANES), f32)
    sums = pltpu.VMEM((4 * TOK, PIECE), bf16)
    scratch = [
        pltpu.VMEM((3, TOK, CHAN), bf16),
        pltpu.VMEM((3, 3, CHAN), f32),
        pltpu.VMEM((MODES, CHAN), f32),
        pltpu.VMEM((MODES, CHAN), f32),
        pltpu.VMEM((GROUPS, LANES), f32),
        pltpu.VMEM((ROWS, 4096), bf16),
        pltpu.VMEM((4, XS, ROWS, PIECE), bf16),
        pltpu.VMEM((XS, CHAN, PIECE), bf16),
        pltpu.VMEM((8, CHAN), f32),
        pltpu.VMEM((8, CHAN), f32),
        pltpu.VMEM((GROUPS * TOK, LANES), f32),
        pltpu.VMEM((TOK, CHAN), f32),
        pltpu.VMEM((GROUPS * TOK, LANES), f32),
        table,
        table,
        table,
        table,
        table,
        table,
        pltpu.VMEM((PLANE, 16, LANES), f32),
        pltpu.VMEM((16, LANES), f32),
        pltpu.VMEM((ZS, 16, LANES), f32),
        pltpu.VMEM((PLANE, 16, LANES), f32),
        table,
        pltpu.VMEM((4 * TOK, CHAN), bf16),
        sums,
        sums,
        sums,
        sums,
        sums,
        sums,
        sums,
        dma,
        dma((8,)),
        dma((1,)),
        dma((1,)),
        dma((2, PLANE)),
        dma((2, PLANE)),
        dma((4, 4)),
        dma((4, 4)),
        dma((4, 4)),
        dma((4, 4)),
        dma((PLANE,)),
        dma((PLANE,)),
        dma((ZS,)),
        dma((ZS,)),
        dma((PLANE,)),
        dma((PLANE,)),
        dma((3, 3)),
        dma((3, 3)),
        dma((5, 4)),
        dma((5, 4)),
        dma((5, 2, 2)),
        dma((2, 4, 4)),
    ]
    halves = pl.pallas_call(
        block_kernel,
        out_shape=jax.ShapeDtypeStruct((2, TOK, 2 * PIECE), bf16),
        in_specs=[pl.BlockSpec(memory_space=pltpu.HBM)] * 6,
        out_specs=pl.BlockSpec(memory_space=pltpu.HBM),
        scratch_shapes=scratch,
        compiler_params=pltpu.CompilerParams(
            collective_id=0, has_side_effects=True, vmem_limit_bytes=61 * 1024 * 1024
        ),
    )(
        projected,
        short_filter,
        decay_rate.T,
        residue.T,
        skip_gain.reshape(GROUPS, LANES),
        out_weight,
    )
    return (halves[0].astype(f32) + halves[1].astype(f32)).astype(bf16)


def solution(mesh):
    in_specs = (
        P(None, "ctx", "tp"),
        P(None, None, "tp"),
        P("tp", None),
        P("tp", None),
        P("tp"),
        P(("tp", "ctx"), None),
    )
    out_specs = P("ctx", "tp")
    return jax.shard_map(
        on_device, mesh=mesh, in_specs=in_specs, out_specs=out_specs, check_vma=False
    )
```

```python
import jax
import jax.numpy as jnp
from jax import lax
from jax.experimental import pallas as pl
from jax.experimental.pallas import tpu as pltpu
from jax.sharding import PartitionSpec as P

ZS = 8
PLANE = 8
XS = 4
TOK = 256
CHAN = 1024
LANES = 128
GROUPS = CHAN // LANES
MODES = 16
ROWS = 16
BLOCK = PLANE * ROWS
ORDER = (2, 1, 3, 0)
PIECE = 256
HEAD = 8
PARTS = ((0, 128), (128, 64), (192, 64))


def block_kernel(
    proj_hbm,
    filt_hbm,
    rate_hbm,
    resid_hbm,
    skip_hbm,
    weight_hbm,
    out,
    proj,
    filt,
    rate,
    resid,
    skip,
    weight,
    wq,
    wbuf,
    halo_out,
    halo_in,
    gates,
    query,
    conv,
    decay,
    gain,
    power,
    late,
    head,
    state,
    stage1,
    total,
    stage2,
    carries,
    carry,
    mixed,
    far_out,
    up_out,
    down_out,
    far_in,
    up_in,
    down_in,
    half_out,
    stay_sem,
    load_sem,
    halo_send,
    halo_recv,
    wy_send,
    wy_recv,
    up_send,
    up_recv,
    dn_send,
    dn_recv,
    s1_send,
    s1_recv,
    s2_send,
    s2_recv,
    s3_send,
    s3_recv,
    mix_send,
    mix_recv,
    x_send,
    x_recv,
    h_send,
    h_recv,
):
    ctx = lax.axis_index("ctx")
    tp = lax.axis_index("tp")
    z = ctx // PLANE
    e = ctx % PLANE
    c = e % 2
    par = (e // 2) % 2
    quad = e // 4
    x = tp // 2
    h = tp % 2

    def at(zz, ee):
        return zz * PLANE + ee

    def partner(k):
        return ((e // 4 + k // 4) % 2) * 4 + ((e // 2 + k // 2) % 2) * 2 + (e + k) % 2

    def member(pp, cc):
        return z * PLANE + quad * 4 + pp * 2 + cc

    def remote(src, dst, send, recv, to_ctx, to_tp):
        return pltpu.make_async_remote_copy(
            src_ref=src,
            dst_ref=dst,
            send_sem=send,
            recv_sem=recv,
            device_id={"ctx": to_ctx, "tp": to_tp},
            device_id_type=pl.DeviceIdType.MESH,
        )

    sent = []

    def start(*args):
        copy = remote(*args)
        copy.start()
        sent.append(copy)

    def arrived(dst, recv):
        remote(dst, dst, recv, recv, at((z + 1) % ZS, e), tp).wait_recv()

    barrier = pltpu.get_barrier_semaphore()

    def greet(to_ctx, to_tp):
        pl.semaphore_signal(
            barrier,
            inc=1,
            device_id={"ctx": to_ctx, "tp": to_tp},
            device_id_type=pl.DeviceIdType.MESH,
        )

    for k in range(1, PLANE):
        greet(at(z, (e + k) % PLANE), tp)
    for k in range(1, ZS):
        greet(at((z + k) % ZS, e), tp)
    for k in (1, XS - 1):
        greet(ctx, ((x + k) % XS) * 2 + h)
    for pp in range(2):
        for cc in range(2):
            greet(member(pp, cc), x * 2 + (1 - h))
    to_next = jnp.logical_and(e == PLANE - 1, z < ZS - 1)
    to_prev = jnp.logical_and(e == 0, z > 0)

    @pl.when(to_next)
    def _():
        greet(ctx + 1, tp)

    @pl.when(to_prev)
    def _():
        greet(ctx - 1, tp)

    loads = [
        pltpu.make_async_copy(src, dst, load_sem.at[k])
        for k, (src, dst) in enumerate(
            [
                (weight_hbm, weight),
                (proj_hbm.at[1], proj.at[1]),
                (proj_hbm.at[2], proj.at[2]),
                (proj_hbm.at[0], proj.at[0]),
                (rate_hbm, rate),
                (filt_hbm, filt),
                (resid_hbm, resid),
                (skip_hbm, skip),
            ]
        )
    ]
    for copy in loads:
        copy.start()

    loads[0].wait()
    for q in range(4):
        pp, cc = q // 2, q % 2
        for j in range(XS):
            for hh in range(2):
                col = (x + ORDER[j]) % XS * 1024 + hh * 512 + (pp * 2 + cc) * LANES
                wq[q, j, :, hh * LANES : (hh + 1) * LANES] = weight[
                    :, pl.ds(pl.multiple_of(col, LANES), LANES)
                ]
    for k in range(1, 4):
        loads[k].wait()
    for p in range(3):
        rim = proj[p, TOK - 16 : TOK, :].astype(jnp.float32)
        halo_out[2 * p : 2 * p + 2, :] = rim[14:16, :]
    halo_out[6:8, :] = jnp.zeros((2, CHAN), jnp.float32)

    @pl.when(ctx == 0)
    def _():
        halo_in[...] = jnp.zeros_like(halo_in)

    beyond = jnp.logical_or(to_next, to_prev).astype(jnp.int32)
    pl.semaphore_wait(barrier, 7 + 7 + 2 + 4 + beyond)

    halo_copy = remote(halo_out, halo_in, halo_send.at[0], halo_recv.at[0], ctx + 1, tp)

    @pl.when(ctx < ZS * PLANE - 1)
    def _():
        halo_copy.start()

    my_rows = pl.ds(pl.multiple_of(z * BLOCK + e * ROWS, ROWS), ROWS)
    groups = (pl.ds(0, 3), pl.ds(3, 1))

    def plane_shares(group):
        js = groups[group]
        for k in range(1, PLANE):
            ee = partner(k)
            share = ((ee // 2) % 2) * 2 + ee % 2
            start(
                wq.at[share, js],
                wbuf.at[js, my_rows],
                wy_send.at[group, k],
                wy_recv.at[group, k],
                at(z, ee),
                tp,
            )

    plane_shares(0)
    wbuf[:, my_rows, :] = wq[par * 2 + c]

    def piece(zz, j):
        return wbuf.at[j, pl.ds(pl.multiple_of(zz * BLOCK, BLOCK), BLOCK)]

    def up_hops(j):
        return 4 - j % 2

    def down_hops(j):
        return 3 + j % 2

    def pass_on(j, s):
        if s < up_hops(j):
            block = piece((z + ZS - s) % ZS, j)
            start(block, block, up_send.at[s, j], up_recv.at[s, j], at((z + 1) % ZS, e), tp)
        if s < down_hops(j):
            block = piece((z + s) % ZS, j)
            start(block, block, dn_send.at[s, j], dn_recv.at[s, j], at((z + ZS - 1) % ZS, e), tp)

    def begin(group):
        for k in range(1, PLANE):
            rows = pl.ds(pl.multiple_of(z * BLOCK + partner(k) * ROWS, ROWS), ROWS)
            arrived(wbuf.at[groups[group], rows], wy_recv.at[group, k])
        for j in (range(3), range(3, 4))[group]:
            pass_on(j, 0)

    def forward(j, s):
        if s < up_hops(j):
            arrived(piece((z + 2 * ZS - 1 - s) % ZS, j), up_recv.at[s, j])
        if s < down_hops(j):
            arrived(piece((z + 1 + s) % ZS, j), dn_recv.at[s, j])
        pass_on(j, s + 1)

    for k in range(4, 8):
        loads[k].wait()
    for g in range(GROUPS):
        cols = slice(g * LANES, (g + 1) * LANES)
        places = pl.ds(g, MODES, stride=GROUPS)
        decay[places, :] = jnp.exp(-rate[:, cols])
        late[places, :] = jnp.exp(rate[:, cols] * (-float(TOK - HEAD)))
        power[places, :] = rate[:, cols]
        gain[places, :] = resid[:, cols]

    row_id = lax.broadcasted_iota(jnp.int32, (TOK, LANES), 0)

    def featured_part(p, cols):
        now = proj[p, :, cols].astype(jnp.float32)
        taps = filt[p, :, cols]
        one = jnp.where(row_id >= 1, pltpu.roll(now, 1, 0), 0.0)
        two = jnp.where(row_id >= 2, pltpu.roll(now, 2, 0), 0.0)
        return taps[0:1, :] * now + taps[1:2, :] * one + taps[2:3, :] * two

    def featurize_gates(g, carry_in):
        cols = pl.ds(pl.multiple_of(g * LANES, LANES), LANES)
        gates[pl.ds(pl.multiple_of(g * TOK, TOK), TOK), :] = (
            (featured_part(1, cols) * featured_part(2, cols)).astype(jnp.bfloat16)
        ).astype(jnp.float32)
        return carry_in

    def featurize_query(g, carry_in):
        cols = pl.ds(pl.multiple_of(g * LANES, LANES), LANES)
        query[:, cols] = featured_part(0, cols)
        return carry_in

    lax.fori_loop(0, GROUPS, featurize_gates, 0)

    def token(ref, t):
        return ref[pl.ds(t, GROUPS, stride=TOK), :]

    def mode(ref, n):
        return ref[n * GROUPS : (n + 1) * GROUPS, :]

    def summed(terms):
        while len(terms) > 1:
            terms = [
                terms[i] + terms[i + 1] if i + 1 < len(terms) else terms[i]
                for i in range(0, len(terms), 2)
            ]
        return terms[0]

    zero = tuple(jnp.zeros((GROUPS, LANES), jnp.float32) for _ in range(MODES))

    def local_filter(step, held):
        for u in range(HEAD):
            t = step * HEAD + u
            g_now = token(gates, t)
            held = tuple(mode(decay, n) * held[n] + g_now for n in range(MODES))
            terms = [mode(gain, n) * held[n] for n in range(MODES)]
            conv[pl.ds(t, GROUPS, stride=TOK), :] = summed(terms + [skip[...] * g_now])
        return held

    steps = TOK // HEAD
    tail = lax.fori_loop(1, steps // 2, local_filter, zero)
    tail = lax.fori_loop(steps // 2, steps, local_filter, tail)
    for n in range(MODES):
        state[n * GROUPS : (n + 1) * GROUPS, :] = tail[n]

    @pl.when(ctx > 0)
    def _():
        remote(halo_in, halo_in, halo_send.at[0], halo_recv.at[0], ctx - 1, tp).wait_recv()

    edge_id = lax.broadcasted_iota(jnp.int32, (HEAD, CHAN), 0)
    featured = []
    for p in range(3):
        now = proj[p, 0:16, :].astype(jnp.float32)[0:HEAD, :]
        before2 = halo_in[2 * p : 2 * p + 1, :]
        before1 = halo_in[2 * p + 1 : 2 * p + 2, :]
        one = jnp.where(edge_id >= 1, pltpu.roll(now, 1, 0), before1)
        two = jnp.where(
            edge_id >= 2, pltpu.roll(now, 2, 0), jnp.where(edge_id == 0, before2, before1)
        )
        taps = filt[p]
        featured.append(taps[0:1, :] * now + taps[1:2, :] * one + taps[2:3, :] * two)
    first = (featured[1] * featured[2]).astype(jnp.bfloat16).astype(jnp.float32)
    for g in range(GROUPS):
        gates[g * TOK : g * TOK + HEAD, :] = first[:, g * LANES : (g + 1) * LANES]
    opening = lax.fori_loop(0, 1, local_filter, zero)
    for n in range(MODES):
        rows = slice(n * GROUPS, (n + 1) * GROUPS)
        head[rows, :] = opening[n]
        state[rows, :] = state[rows, :] + late[rows, :] * opening[n]

    own_modes = pl.ds(pl.multiple_of(e * 16, 16), 16)
    for k in range(1, PLANE):
        ee = (e + k) % PLANE
        start(
            state.at[pl.ds(pl.multiple_of(ee * 16, 16), 16)],
            stage1.at[e],
            s1_send.at[k],
            s1_recv.at[k],
            at(z, ee),
            tp,
        )
    stage1[e] = state[own_modes, :]

    lax.fori_loop(0, GROUPS, featurize_query, 0)
    query[0:HEAD, :] = featured[0]
    begin(0)
    plane_shares(1)
    forward(0, 0)

    for k in range(1, PLANE):
        arrived(stage1.at[(e + PLANE - k) % PLANE], s1_recv.at[k])
    rates = power[own_modes, :]
    over_device = jnp.exp(rates * (-float(TOK)))
    over_plane = jnp.exp(rates * (-float(TOK * PLANE)))
    running = stage1[0]
    for k in range(1, PLANE):
        running = over_device * running + stage1[k]
    total[...] = running
    for k in range(1, ZS):
        start(total, stage2.at[z], s2_send.at[k], s2_recv.at[k], at((z + k) % ZS, e), tp)
    stage2[z] = running

    forward(1, 0)
    forward(2, 0)
    forward(0, 1)

    for k in range(1, ZS):
        arrived(stage2.at[(z + ZS - k) % ZS], s2_recv.at[k])
    running = jnp.zeros((16, LANES), jnp.float32)
    for k in range(ZS - 1):
        running = jnp.where(k < z, over_plane * running + stage2[k], running)
    for k in range(PLANE):
        carries[k] = running
        if k < PLANE - 1:
            running = over_device * running + stage1[k]
    for k in range(1, PLANE):
        ee = (e + k) % PLANE
        start(carries.at[ee], carry.at[own_modes], s3_send.at[k], s3_recv.at[k], at(z, ee), tp)
    carry[own_modes, :] = carries[e]

    forward(1, 1)
    forward(2, 1)
    forward(0, 2)
    begin(1)

    for k in range(1, PLANE):
        ee = (e + PLANE - k) % PLANE
        arrived(carry.at[pl.ds(pl.multiple_of(ee * 16, 16), 16)], s3_recv.at[k])

    def add_carry(step, held):
        for u in range(HEAD):
            t = step * HEAD + u
            held = tuple(mode(decay, n) * held[n] for n in range(MODES))
            conv[pl.ds(t, GROUPS, stride=TOK), :] = summed(list(held) + [token(conv, t)])
        return held

    across = member(1 - par, c)
    sibling = member(par, 1 - c)

    def direct(part):
        first, count = PARTS[part]
        return pl.ds(2 * TOK + 2 * first, count)

    def indirect(part):
        first, count = PARTS[part]
        return pl.ds(2 * TOK + 2 * first + count, count)

    def mix(part):
        first, count = PARTS[part]
        rows = slice(first, first + count)

        def mix_group(g, carry_in):
            cols = pl.ds(pl.multiple_of(g * LANES, LANES), LANES)
            places = pl.ds(pl.multiple_of(g * TOK + first, count), count)
            filtered = conv[places, :].astype(jnp.bfloat16).astype(jnp.float32)
            mixed[rows, cols] = (query[rows, cols] * filtered).astype(jnp.bfloat16)
            return carry_in

        lax.fori_loop(0, GROUPS, mix_group, 0)
        mine = mixed.at[pl.ds(first, count)]
        there = mixed.at[direct(part)]
        start(mine, there, mix_send.at[part, 0], mix_recv.at[part, 0], across, tp)
        there = mixed.at[pl.ds(TOK + first, count)]
        start(mine, there, mix_send.at[part, 1], mix_recv.at[part, 1], sibling, tp)

    held = tuple(mode(gain, n) * mode(carry, n) for n in range(MODES))
    held = lax.fori_loop(0, 1, add_carry, held)
    held = tuple(held[n] + mode(gain, n) * mode(head, n) for n in range(MODES))
    held = lax.fori_loop(1, steps // 2, add_carry, held)
    mix(0)
    held = lax.fori_loop(steps // 2, steps * 3 // 4, add_carry, held)
    mix(1)
    lax.fori_loop(steps * 3 // 4, steps, add_carry, held)
    mix(2)
    forward(1, 2)
    forward(2, 2)
    forward(0, 3)

    chunks = [(0, TOK), (TOK, TOK)] + [(2 * TOK + 2 * first, 2 * count) for first, count in PARTS]

    def product(m, d):
        first, count = chunks[m]
        return jnp.dot(
            mixed[first : first + count, :],
            wbuf[ORDER.index(d)],
            preferred_element_type=jnp.float32,
        )

    right = ((x + 1) % XS) * 2 + h
    left = ((x + XS - 1) % XS) * 2 + h

    def spans(m):
        first, count = chunks[m]
        half = count // 2
        return pl.ds(first, count), pl.ds(first, half), pl.ds(first + half, half), half

    def far_terms(m):
        every, upper, lower, _ = spans(m)
        far_out[every, :] = product(m, 2).astype(jnp.bfloat16)
        into = far_in.at[upper]
        start(far_out.at[upper], into, x_send.at[m, 0], x_recv.at[m, 0], ctx, right)
        into = far_in.at[lower]
        start(far_out.at[lower], into, x_send.at[m, 1], x_recv.at[m, 1], ctx, left)

    def near_terms(m):
        every, upper, lower, half = spans(m)
        term = product(m, 1)
        up_out[lower, :] = term[half:].astype(jnp.bfloat16)
        arrived(far_in.at[upper], x_recv.at[m, 0])
        up_out[upper, :] = (term[:half] + far_in[upper, :].astype(jnp.float32)).astype(jnp.bfloat16)
        start(up_out.at[every], up_in.at[every], x_send.at[m, 2], x_recv.at[m, 2], ctx, right)
        term = product(m, 3)
        down_out[upper, :] = term[:half].astype(jnp.bfloat16)
        arrived(far_in.at[lower], x_recv.at[m, 1])
        down_out[lower, :] = (term[half:] + far_in[lower, :].astype(jnp.float32)).astype(
            jnp.bfloat16
        )
        start(down_out.at[every], down_in.at[every], x_send.at[m, 3], x_recv.at[m, 3], ctx, left)

    last = []
    my_columns = pl.ds(pl.multiple_of((par * 2 + c) * LANES, LANES), LANES)

    def of_half(hh):
        return pl.ds(pl.multiple_of(hh * LANES, LANES), LANES)

    stay = pltpu.make_async_copy(
        half_out.at[pl.ds(0, TOK), of_half(h)], out.at[h, :, my_columns], stay_sem
    )

    def own_terms(m):
        every, upper, lower, half = spans(m)
        term = product(m, 0)
        arrived(up_in.at[every], x_recv.at[m, 2])
        arrived(down_in.at[every], x_recv.at[m, 3])
        both = up_in[every, :].astype(jnp.float32) + down_in[every, :].astype(jnp.float32)
        half_out[every, :] = (term + both).astype(jnp.bfloat16)
        if m < 2:
            moves = [(member(par, (c + m) % 2), every, pl.ds(0, TOK), 3)]
        else:
            place = pl.ds(*PARTS[m - 2])
            moves = [
                (member(1 - par, c), upper, place, m - 2),
                (member(1 - par, 1 - c), lower, place, m - 2),
            ]
        for a in (1, 0):
            hh = (h + a) % 2
            for k, (to, rows, place, slot) in enumerate(moves):
                if m == 0 and a == 0:
                    stay.start()
                    continue
                copy = remote(
                    half_out.at[rows, of_half(hh)],
                    out.at[h, place, my_columns],
                    h_send.at[m, a, k],
                    h_recv.at[h, par * 2 + c, slot],
                    to,
                    x * 2 + hh,
                )
                copy.start()
                last.append(copy)

    def from_across(part):
        rows = direct(part)
        arrived(mixed.at[rows], mix_recv.at[part, 0])
        there = mixed.at[indirect(part)]
        start(mixed.at[rows], there, mix_send.at[part, 2], mix_recv.at[part, 2], sibling, tp)

    def from_sibling(part):
        arrived(mixed.at[indirect(part)], mix_recv.at[part, 2])

    far_terms(0)
    for part, (first, count) in enumerate(PARTS):
        arrived(mixed.at[pl.ds(TOK + first, count)], mix_recv.at[part, 1])
    far_terms(1)
    forward(3, 0)
    forward(1, 3)
    forward(2, 3)
    near_terms(0)
    forward(3, 1)
    from_across(0)
    near_terms(1)
    forward(3, 2)
    from_sibling(0)
    far_terms(2)
    from_across(1)
    forward(3, 3)
    own_terms(0)
    from_sibling(1)
    far_terms(3)
    from_across(2)
    near_terms(2)
    from_sibling(2)
    far_terms(4)
    own_terms(1)
    near_terms(3)
    near_terms(4)
    own_terms(2)
    own_terms(3)
    own_terms(4)

    for k in range(8):
        hs, ps, cs = (h + k // 4) % 2, (par + k // 2) % 2, (c + k) % 2
        columns = pl.ds(pl.multiple_of((ps * 2 + cs) * LANES, LANES), LANES)
        if k == 0:
            stay.wait()
        elif k // 2 % 2 == 0:
            arrived(out.at[hs, :, columns], h_recv.at[hs, ps * 2 + cs, 3])
        else:
            for part, (first, count) in enumerate(PARTS):
                place = out.at[hs, pl.ds(first, count), columns]
                arrived(place, h_recv.at[hs, ps * 2 + cs, part])

    @pl.when(ctx < ZS * PLANE - 1)
    def _():
        halo_copy.wait_send()

    for copy in sent:
        copy.wait_send()
    for copy in last:
        copy.wait_send()


def on_device(projected, short_filter, decay_rate, residue, skip_gain, out_weight):
    f32, bf16 = jnp.float32, jnp.bfloat16
    dma = pltpu.SemaphoreType.DMA
    table = pltpu.VMEM(((MODES + 1) * GROUPS, LANES), f32)
    by_token = pltpu.VMEM(((GROUPS + 1) * TOK, LANES), f32)
    sums = pltpu.VMEM((4 * TOK, PIECE), bf16)
    scratch = [
        pltpu.VMEM((3, TOK, CHAN), bf16),
        pltpu.VMEM((3, 3, CHAN), f32),
        pltpu.VMEM((MODES, CHAN), f32),
        pltpu.VMEM((MODES, CHAN), f32),
        pltpu.VMEM((GROUPS, LANES), f32),
        pltpu.VMEM((ROWS, 4096), bf16),
        pltpu.VMEM((4, XS, ROWS, PIECE), bf16),
        pltpu.VMEM((XS, CHAN, PIECE), bf16),
        pltpu.VMEM((8, CHAN), f32),
        pltpu.VMEM((8, CHAN), f32),
        by_token,
        pltpu.VMEM((TOK, CHAN), f32),
        by_token,
        table,
        table,
        table,
        table,
        table,
        table,
        pltpu.VMEM((PLANE, 16, LANES), f32),
        pltpu.VMEM((16, LANES), f32),
        pltpu.VMEM((ZS, 16, LANES), f32),
        pltpu.VMEM((PLANE, 16, LANES), f32),
        table,
        pltpu.VMEM((4 * TOK, CHAN), bf16),
        sums,
        sums,
        sums,
        sums,
        sums,
        sums,
        sums,
        dma,
        dma((8,)),
        dma((1,)),
        dma((1,)),
        dma((2, PLANE)),
        dma((2, PLANE)),
        dma((4, 4)),
        dma((4, 4)),
        dma((4, 4)),
        dma((4, 4)),
        dma((PLANE,)),
        dma((PLANE,)),
        dma((ZS,)),
        dma((ZS,)),
        dma((PLANE,)),
        dma((PLANE,)),
        dma((3, 3)),
        dma((3, 3)),
        dma((5, 4)),
        dma((5, 4)),
        dma((5, 2, 2)),
        dma((2, 4, 4)),
    ]
    halves = pl.pallas_call(
        block_kernel,
        out_shape=jax.ShapeDtypeStruct((2, TOK, 2 * PIECE), bf16),
        in_specs=[pl.BlockSpec(memory_space=pltpu.HBM)] * 6,
        out_specs=pl.BlockSpec(memory_space=pltpu.HBM),
        scratch_shapes=scratch,
        compiler_params=pltpu.CompilerParams(
            collective_id=0, has_side_effects=True, vmem_limit_bytes=61 * 1024 * 1024
        ),
    )(
        projected,
        short_filter,
        decay_rate.T,
        residue.T,
        skip_gain.reshape(GROUPS, LANES),
        out_weight,
    )
    return (halves[0].astype(f32) + halves[1].astype(f32)).astype(bf16)


def solution(mesh):
    in_specs = (
        P(None, "ctx", "tp"),
        P(None, None, "tp"),
        P("tp", None),
        P("tp", None),
        P("tp"),
        P(("tp", "ctx"), None),
    )
    out_specs = P("ctx", "tp")
    return jax.shard_map(
        on_device, mesh=mesh, in_specs=in_specs, out_specs=out_specs, check_vma=False
    )
```

```python
import jax
import jax.numpy as jnp
from jax import lax
from jax.experimental import pallas as pl
from jax.experimental.pallas import tpu as pltpu
from jax.sharding import PartitionSpec as P

ZS = 8
PLANE = 8
XS = 4
TOK = 256
CHAN = 1024
LANES = 128
GROUPS = CHAN // LANES
MODES = 16
ROWS = 16
BLOCK = PLANE * ROWS
ORDER = (2, 1, 3, 0)
PIECE = 256
HEAD = 8
PARTS = ((0, 128), (128, 64), (192, 64))


def block_kernel(
    proj_hbm,
    filt_hbm,
    rate_hbm,
    resid_hbm,
    skip_hbm,
    weight_hbm,
    out,
    proj,
    rims,
    filt,
    rate,
    resid,
    skip,
    weight,
    wq,
    wbuf,
    halo_out,
    halo_in,
    gates,
    query,
    conv,
    decay,
    gain,
    power,
    late,
    head,
    state,
    stage1,
    total,
    stage2,
    carries,
    carry,
    mixed,
    far_out,
    up_out,
    down_out,
    far_in,
    up_in,
    down_in,
    half_out,
    stay_sem,
    load_sem,
    halo_send,
    halo_recv,
    wy_send,
    wy_recv,
    up_send,
    up_recv,
    dn_send,
    dn_recv,
    s1_send,
    s1_recv,
    s2_send,
    s2_recv,
    s3_send,
    s3_recv,
    mix_send,
    mix_recv,
    x_send,
    x_recv,
    h_send,
    h_recv,
):
    ctx = lax.axis_index("ctx")
    tp = lax.axis_index("tp")
    z = ctx // PLANE
    e = ctx % PLANE
    c = e % 2
    par = (e // 2) % 2
    quad = e // 4
    x = tp // 2
    h = tp % 2

    def at(zz, ee):
        return zz * PLANE + ee

    def partner(k):
        return ((e // 4 + k // 4) % 2) * 4 + ((e // 2 + k // 2) % 2) * 2 + (e + k) % 2

    def member(pp, cc):
        return z * PLANE + quad * 4 + pp * 2 + cc

    def remote(src, dst, send, recv, to_ctx, to_tp):
        return pltpu.make_async_remote_copy(
            src_ref=src,
            dst_ref=dst,
            send_sem=send,
            recv_sem=recv,
            device_id={"ctx": to_ctx, "tp": to_tp},
            device_id_type=pl.DeviceIdType.MESH,
        )

    sent = []

    def start(*args):
        copy = remote(*args)
        copy.start()
        sent.append(copy)

    def arrived(dst, recv):
        remote(dst, dst, recv, recv, at((z + 1) % ZS, e), tp).wait_recv()

    barrier = pltpu.get_barrier_semaphore()

    def greet(to_ctx, to_tp):
        pl.semaphore_signal(
            barrier,
            inc=1,
            device_id={"ctx": to_ctx, "tp": to_tp},
            device_id_type=pl.DeviceIdType.MESH,
        )

    for k in range(1, PLANE):
        greet(at(z, (e + k) % PLANE), tp)
    for k in range(1, ZS):
        greet(at((z + k) % ZS, e), tp)
    for k in (1, XS - 1):
        greet(ctx, ((x + k) % XS) * 2 + h)
    for pp in range(2):
        for cc in range(2):
            greet(member(pp, cc), x * 2 + (1 - h))
    to_next = jnp.logical_and(e == PLANE - 1, z < ZS - 1)
    to_prev = jnp.logical_and(e == 0, z > 0)

    @pl.when(to_next)
    def _():
        greet(ctx + 1, tp)

    @pl.when(to_prev)
    def _():
        greet(ctx - 1, tp)

    loads = [
        pltpu.make_async_copy(src, dst, load_sem.at[k])
        for k, (src, dst) in enumerate(
            [
                (weight_hbm, weight),
                (proj_hbm.at[:, pl.ds(TOK - 16, 16)], rims),
                (proj_hbm.at[1], proj.at[1]),
                (proj_hbm.at[2], proj.at[2]),
                (proj_hbm.at[0], proj.at[0]),
                (rate_hbm, rate),
                (filt_hbm, filt),
                (resid_hbm, resid),
                (skip_hbm, skip),
            ]
        )
    ]
    for copy in loads:
        copy.start()

    loads[0].wait()
    for q in range(4):
        pp, cc = q // 2, q % 2
        for j in range(XS):
            for hh in range(2):
                col = (x + ORDER[j]) % XS * 1024 + hh * 512 + (pp * 2 + cc) * LANES
                wq[q, j, :, hh * LANES : (hh + 1) * LANES] = weight[
                    :, pl.ds(pl.multiple_of(col, LANES), LANES)
                ]
    loads[1].wait()
    for p in range(3):
        rim = rims[p].astype(jnp.float32)
        halo_out[2 * p : 2 * p + 2, :] = rim[14:16, :]
    halo_out[6:8, :] = jnp.zeros((2, CHAN), jnp.float32)

    @pl.when(ctx == 0)
    def _():
        halo_in[...] = jnp.zeros_like(halo_in)

    beyond = jnp.logical_or(to_next, to_prev).astype(jnp.int32)
    pl.semaphore_wait(barrier, 7 + 7 + 2 + 4 + beyond)

    halo_copy = remote(halo_out, halo_in, halo_send.at[0], halo_recv.at[0], ctx + 1, tp)

    @pl.when(ctx < ZS * PLANE - 1)
    def _():
        halo_copy.start()

    my_rows = pl.ds(pl.multiple_of(z * BLOCK + e * ROWS, ROWS), ROWS)
    groups = (pl.ds(0, 3), pl.ds(3, 1))

    def plane_shares(group):
        js = groups[group]
        for k in range(1, PLANE):
            ee = partner(k)
            share = ((ee // 2) % 2) * 2 + ee % 2
            start(
                wq.at[share, js],
                wbuf.at[js, my_rows],
                wy_send.at[group, k],
                wy_recv.at[group, k],
                at(z, ee),
                tp,
            )

    plane_shares(0)
    wbuf[:, my_rows, :] = wq[par * 2 + c]

    def piece(zz, j):
        return wbuf.at[j, pl.ds(pl.multiple_of(zz * BLOCK, BLOCK), BLOCK)]

    def up_hops(j):
        return 4 - j % 2

    def down_hops(j):
        return 3 + j % 2

    def pass_on(j, s):
        if s < up_hops(j):
            block = piece((z + ZS - s) % ZS, j)
            start(block, block, up_send.at[s, j], up_recv.at[s, j], at((z + 1) % ZS, e), tp)
        if s < down_hops(j):
            block = piece((z + s) % ZS, j)
            start(block, block, dn_send.at[s, j], dn_recv.at[s, j], at((z + ZS - 1) % ZS, e), tp)

    def begin(group):
        for k in range(1, PLANE):
            rows = pl.ds(pl.multiple_of(z * BLOCK + partner(k) * ROWS, ROWS), ROWS)
            arrived(wbuf.at[groups[group], rows], wy_recv.at[group, k])
        for j in (range(3), range(3, 4))[group]:
            pass_on(j, 0)

    def forward(j, s):
        if s < up_hops(j):
            arrived(piece((z + 2 * ZS - 1 - s) % ZS, j), up_recv.at[s, j])
        if s < down_hops(j):
            arrived(piece((z + 1 + s) % ZS, j), dn_recv.at[s, j])
        pass_on(j, s + 1)

    for k in range(2, 9):
        loads[k].wait()
    for g in range(GROUPS):
        cols = slice(g * LANES, (g + 1) * LANES)
        places = pl.ds(g, MODES, stride=GROUPS)
        decay[places, :] = jnp.exp(-rate[:, cols])
        late[places, :] = jnp.exp(rate[:, cols] * (-float(TOK - HEAD)))
        power[places, :] = rate[:, cols]
        gain[places, :] = resid[:, cols]

    row_id = lax.broadcasted_iota(jnp.int32, (TOK, LANES), 0)

    def featured_part(p, cols):
        now = proj[p, :, cols].astype(jnp.float32)
        taps = filt[p, :, cols]
        one = jnp.where(row_id >= 1, pltpu.roll(now, 1, 0), 0.0)
        two = jnp.where(row_id >= 2, pltpu.roll(now, 2, 0), 0.0)
        return taps[0:1, :] * now + taps[1:2, :] * one + taps[2:3, :] * two

    def featurize_gates(g, carry_in):
        cols = pl.ds(pl.multiple_of(g * LANES, LANES), LANES)
        gates[pl.ds(pl.multiple_of(g * TOK, TOK), TOK), :] = (
            (featured_part(1, cols) * featured_part(2, cols)).astype(jnp.bfloat16)
        ).astype(jnp.float32)
        return carry_in

    def featurize_query(g, carry_in):
        cols = pl.ds(pl.multiple_of(g * LANES, LANES), LANES)
        query[:, cols] = featured_part(0, cols)
        return carry_in

    lax.fori_loop(0, GROUPS, featurize_gates, 0)

    def token(ref, t):
        return ref[pl.ds(t, GROUPS, stride=TOK), :]

    def mode(ref, n):
        return ref[n * GROUPS : (n + 1) * GROUPS, :]

    def summed(terms):
        while len(terms) > 1:
            terms = [
                terms[i] + terms[i + 1] if i + 1 < len(terms) else terms[i]
                for i in range(0, len(terms), 2)
            ]
        return terms[0]

    zero = tuple(jnp.zeros((GROUPS, LANES), jnp.float32) for _ in range(MODES))

    def local_filter(step, held):
        for u in range(HEAD):
            t = step * HEAD + u
            g_now = token(gates, t)
            held = tuple(mode(decay, n) * held[n] + g_now for n in range(MODES))
            terms = [mode(gain, n) * held[n] for n in range(MODES)]
            conv[pl.ds(t, GROUPS, stride=TOK), :] = summed(terms + [skip[...] * g_now])
        return held

    steps = TOK // HEAD
    tail = lax.fori_loop(1, steps // 2, local_filter, zero)
    tail = lax.fori_loop(steps // 2, steps, local_filter, tail)
    for n in range(MODES):
        state[n * GROUPS : (n + 1) * GROUPS, :] = tail[n]

    @pl.when(ctx > 0)
    def _():
        remote(halo_in, halo_in, halo_send.at[0], halo_recv.at[0], ctx - 1, tp).wait_recv()

    edge_id = lax.broadcasted_iota(jnp.int32, (HEAD, CHAN), 0)
    featured = []
    for p in range(3):
        now = proj[p, 0:16, :].astype(jnp.float32)[0:HEAD, :]
        before2 = halo_in[2 * p : 2 * p + 1, :]
        before1 = halo_in[2 * p + 1 : 2 * p + 2, :]
        one = jnp.where(edge_id >= 1, pltpu.roll(now, 1, 0), before1)
        two = jnp.where(
            edge_id >= 2, pltpu.roll(now, 2, 0), jnp.where(edge_id == 0, before2, before1)
        )
        taps = filt[p]
        featured.append(taps[0:1, :] * now + taps[1:2, :] * one + taps[2:3, :] * two)
    first = (featured[1] * featured[2]).astype(jnp.bfloat16).astype(jnp.float32)
    for g in range(GROUPS):
        gates[g * TOK : g * TOK + HEAD, :] = first[:, g * LANES : (g + 1) * LANES]
    opening = lax.fori_loop(0, 1, local_filter, zero)
    for n in range(MODES):
        rows = slice(n * GROUPS, (n + 1) * GROUPS)
        head[rows, :] = opening[n]
        state[rows, :] = state[rows, :] + late[rows, :] * opening[n]

    own_modes = pl.ds(pl.multiple_of(e * 16, 16), 16)
    for k in range(1, PLANE):
        ee = (e + k) % PLANE
        start(
            state.at[pl.ds(pl.multiple_of(ee * 16, 16), 16)],
            stage1.at[e],
            s1_send.at[k],
            s1_recv.at[k],
            at(z, ee),
            tp,
        )
    stage1[e] = state[own_modes, :]

    lax.fori_loop(0, GROUPS, featurize_query, 0)
    query[0:HEAD, :] = featured[0]
    begin(0)
    plane_shares(1)
    forward(0, 0)

    for k in range(1, PLANE):
        arrived(stage1.at[(e + PLANE - k) % PLANE], s1_recv.at[k])
    rates = power[own_modes, :]
    over_device = jnp.exp(rates * (-float(TOK)))
    over_plane = jnp.exp(rates * (-float(TOK * PLANE)))
    running = stage1[0]
    for k in range(1, PLANE):
        running = over_device * running + stage1[k]
    total[...] = running
    onward = []
    for k in range(1, ZS):
        copy = remote(total, stage2.at[z], s2_send.at[k], s2_recv.at[k], at((z + k) % ZS, e), tp)
        pl.when(z + k < ZS)(copy.start)
        onward.append((k, copy))
    stage2[z] = running

    forward(1, 0)
    forward(2, 0)
    forward(0, 1)

    for k in range(1, ZS):

        @pl.when(z >= k)
        def _(k=k):
            arrived(stage2.at[(z + ZS - k) % ZS], s2_recv.at[k])

    running = jnp.zeros((16, LANES), jnp.float32)
    for k in range(ZS - 1):
        running = jnp.where(k < z, over_plane * running + stage2[k], running)
    for k in range(PLANE):
        carries[k] = running
        if k < PLANE - 1:
            running = over_device * running + stage1[k]
    for k in range(1, PLANE):
        ee = (e + k) % PLANE
        start(carries.at[ee], carry.at[own_modes], s3_send.at[k], s3_recv.at[k], at(z, ee), tp)
    carry[own_modes, :] = carries[e]

    forward(1, 1)
    forward(2, 1)
    forward(0, 2)
    begin(1)

    for k in range(1, PLANE):
        ee = (e + PLANE - k) % PLANE
        arrived(carry.at[pl.ds(pl.multiple_of(ee * 16, 16), 16)], s3_recv.at[k])

    def add_carry(step, held):
        for u in range(HEAD):
            t = step * HEAD + u
            held = tuple(mode(decay, n) * held[n] for n in range(MODES))
            conv[pl.ds(t, GROUPS, stride=TOK), :] = summed(list(held) + [token(conv, t)])
        return held

    across = member(1 - par, c)
    sibling = member(par, 1 - c)

    def direct(part):
        first, count = PARTS[part]
        return pl.ds(2 * TOK + 2 * first, count)

    def indirect(part):
        first, count = PARTS[part]
        return pl.ds(2 * TOK + 2 * first + count, count)

    def mix(part):
        first, count = PARTS[part]
        rows = slice(first, first + count)

        def mix_group(g, carry_in):
            cols = pl.ds(pl.multiple_of(g * LANES, LANES), LANES)
            places = pl.ds(pl.multiple_of(g * TOK + first, count), count)
            filtered = conv[places, :].astype(jnp.bfloat16).astype(jnp.float32)
            mixed[rows, cols] = (query[rows, cols] * filtered).astype(jnp.bfloat16)
            return carry_in

        lax.fori_loop(0, GROUPS, mix_group, 0)
        mine = mixed.at[pl.ds(first, count)]
        there = mixed.at[direct(part)]
        start(mine, there, mix_send.at[part, 0], mix_recv.at[part, 0], across, tp)
        there = mixed.at[pl.ds(TOK + first, count)]
        start(mine, there, mix_send.at[part, 1], mix_recv.at[part, 1], sibling, tp)

    held = tuple(mode(gain, n) * mode(carry, n) for n in range(MODES))
    held = lax.fori_loop(0, 1, add_carry, held)
    held = tuple(held[n] + mode(gain, n) * mode(head, n) for n in range(MODES))
    held = lax.fori_loop(1, steps // 2, add_carry, held)
    mix(0)
    held = lax.fori_loop(steps // 2, steps * 3 // 4, add_carry, held)
    mix(1)
    lax.fori_loop(steps * 3 // 4, steps, add_carry, held)
    mix(2)
    forward(1, 2)
    forward(2, 2)
    forward(0, 3)

    chunks = [(0, TOK), (TOK, TOK)] + [(2 * TOK + 2 * first, 2 * count) for first, count in PARTS]

    def product(m, d):
        first, count = chunks[m]
        return jnp.dot(
            mixed[first : first + count, :],
            wbuf[ORDER.index(d)],
            preferred_element_type=jnp.float32,
        )

    right = ((x + 1) % XS) * 2 + h
    left = ((x + XS - 1) % XS) * 2 + h

    def spans(m):
        first, count = chunks[m]
        half = count // 2
        return pl.ds(first, count), pl.ds(first, half), pl.ds(first + half, half), half

    def far_terms(m):
        every, upper, lower, _ = spans(m)
        far_out[every, :] = product(m, 2).astype(jnp.bfloat16)
        into = far_in.at[upper]
        start(far_out.at[upper], into, x_send.at[m, 0], x_recv.at[m, 0], ctx, right)
        into = far_in.at[lower]
        start(far_out.at[lower], into, x_send.at[m, 1], x_recv.at[m, 1], ctx, left)

    def near_terms(m):
        every, upper, lower, half = spans(m)
        term = product(m, 1)
        up_out[lower, :] = term[half:].astype(jnp.bfloat16)
        arrived(far_in.at[upper], x_recv.at[m, 0])
        up_out[upper, :] = (term[:half] + far_in[upper, :].astype(jnp.float32)).astype(jnp.bfloat16)
        start(up_out.at[every], up_in.at[every], x_send.at[m, 2], x_recv.at[m, 2], ctx, right)
        term = product(m, 3)
        down_out[upper, :] = term[:half].astype(jnp.bfloat16)
        arrived(far_in.at[lower], x_recv.at[m, 1])
        down_out[lower, :] = (term[half:] + far_in[lower, :].astype(jnp.float32)).astype(
            jnp.bfloat16
        )
        start(down_out.at[every], down_in.at[every], x_send.at[m, 3], x_recv.at[m, 3], ctx, left)

    last = []
    my_columns = pl.ds(pl.multiple_of((par * 2 + c) * LANES, LANES), LANES)

    def of_half(hh):
        return pl.ds(pl.multiple_of(hh * LANES, LANES), LANES)

    stay = pltpu.make_async_copy(
        half_out.at[pl.ds(0, TOK), of_half(h)], out.at[h, :, my_columns], stay_sem
    )

    def own_terms(m):
        every, upper, lower, half = spans(m)
        term = product(m, 0)
        arrived(up_in.at[every], x_recv.at[m, 2])
        arrived(down_in.at[every], x_recv.at[m, 3])
        both = up_in[every, :].astype(jnp.float32) + down_in[every, :].astype(jnp.float32)
        half_out[every, :] = (term + both).astype(jnp.bfloat16)
        if m < 2:
            moves = [(member(par, (c + m) % 2), every, pl.ds(0, TOK), 3)]
        else:
            place = pl.ds(*PARTS[m - 2])
            moves = [
                (member(1 - par, c), upper, place, m - 2),
                (member(1 - par, 1 - c), lower, place, m - 2),
            ]
        for a in (1, 0):
            hh = (h + a) % 2
            for k, (to, rows, place, slot) in enumerate(moves):
                if m == 0 and a == 0:
                    stay.start()
                    continue
                copy = remote(
                    half_out.at[rows, of_half(hh)],
                    out.at[h, place, my_columns],
                    h_send.at[m, a, k],
                    h_recv.at[h, par * 2 + c, slot],
                    to,
                    x * 2 + hh,
                )
                copy.start()
                last.append(copy)

    def from_across(part):
        rows = direct(part)
        arrived(mixed.at[rows], mix_recv.at[part, 0])
        there = mixed.at[indirect(part)]
        start(mixed.at[rows], there, mix_send.at[part, 2], mix_recv.at[part, 2], sibling, tp)

    def from_sibling(part):
        arrived(mixed.at[indirect(part)], mix_recv.at[part, 2])

    far_terms(0)
    for part, (first, count) in enumerate(PARTS):
        arrived(mixed.at[pl.ds(TOK + first, count)], mix_recv.at[part, 1])
    far_terms(1)
    forward(3, 0)
    forward(1, 3)
    forward(2, 3)
    near_terms(0)
    forward(3, 1)
    from_across(0)
    near_terms(1)
    forward(3, 2)
    from_sibling(0)
    far_terms(2)
    from_across(1)
    forward(3, 3)
    own_terms(0)
    from_sibling(1)
    far_terms(3)
    from_across(2)
    near_terms(2)
    from_sibling(2)
    far_terms(4)
    own_terms(1)
    near_terms(3)
    near_terms(4)
    own_terms(2)
    own_terms(3)
    own_terms(4)

    for k in range(8):
        hs, ps, cs = (h + k // 4) % 2, (par + k // 2) % 2, (c + k) % 2
        columns = pl.ds(pl.multiple_of((ps * 2 + cs) * LANES, LANES), LANES)
        if k == 0:
            stay.wait()
        elif k // 2 % 2 == 0:
            arrived(out.at[hs, :, columns], h_recv.at[hs, ps * 2 + cs, 3])
        else:
            for part, (first, count) in enumerate(PARTS):
                place = out.at[hs, pl.ds(first, count), columns]
                arrived(place, h_recv.at[hs, ps * 2 + cs, part])

    @pl.when(ctx < ZS * PLANE - 1)
    def _():
        halo_copy.wait_send()

    for copy in sent:
        copy.wait_send()
    for copy in last:
        copy.wait_send()
    for k, copy in onward:
        pl.when(z + k < ZS)(copy.wait_send)


def on_device(projected, short_filter, decay_rate, residue, skip_gain, out_weight):
    f32, bf16 = jnp.float32, jnp.bfloat16
    dma = pltpu.SemaphoreType.DMA
    table = pltpu.VMEM(((MODES + 1) * GROUPS, LANES), f32)
    by_token = pltpu.VMEM(((GROUPS + 1) * TOK, LANES), f32)
    sums = pltpu.VMEM((4 * TOK, PIECE), bf16)
    scratch = [
        pltpu.VMEM((3, TOK, CHAN), bf16),
        pltpu.VMEM((3, 16, CHAN), bf16),
        pltpu.VMEM((3, 3, CHAN), f32),
        pltpu.VMEM((MODES, CHAN), f32),
        pltpu.VMEM((MODES, CHAN), f32),
        pltpu.VMEM((GROUPS, LANES), f32),
        pltpu.VMEM((ROWS, 4096), bf16),
        pltpu.VMEM((4, XS, ROWS, PIECE), bf16),
        pltpu.VMEM((XS, CHAN, PIECE), bf16),
        pltpu.VMEM((8, CHAN), f32),
        pltpu.VMEM((8, CHAN), f32),
        by_token,
        pltpu.VMEM((TOK, CHAN), f32),
        by_token,
        table,
        table,
        table,
        table,
        table,
        table,
        pltpu.VMEM((PLANE, 16, LANES), f32),
        pltpu.VMEM((16, LANES), f32),
        pltpu.VMEM((ZS, 16, LANES), f32),
        pltpu.VMEM((PLANE, 16, LANES), f32),
        table,
        pltpu.VMEM((4 * TOK, CHAN), bf16),
        sums,
        sums,
        sums,
        sums,
        sums,
        sums,
        sums,
        dma,
        dma((9,)),
        dma((1,)),
        dma((1,)),
        dma((2, PLANE)),
        dma((2, PLANE)),
        dma((4, 4)),
        dma((4, 4)),
        dma((4, 4)),
        dma((4, 4)),
        dma((PLANE,)),
        dma((PLANE,)),
        dma((ZS,)),
        dma((ZS,)),
        dma((PLANE,)),
        dma((PLANE,)),
        dma((3, 3)),
        dma((3, 3)),
        dma((5, 4)),
        dma((5, 4)),
        dma((5, 2, 2)),
        dma((2, 4, 4)),
    ]
    halves = pl.pallas_call(
        block_kernel,
        out_shape=jax.ShapeDtypeStruct((2, TOK, 2 * PIECE), bf16),
        in_specs=[pl.BlockSpec(memory_space=pltpu.HBM)] * 6,
        out_specs=pl.BlockSpec(memory_space=pltpu.HBM),
        scratch_shapes=scratch,
        compiler_params=pltpu.CompilerParams(
            collective_id=0, has_side_effects=True, vmem_limit_bytes=61 * 1024 * 1024
        ),
    )(
        projected,
        short_filter,
        decay_rate.T,
        residue.T,
        skip_gain.reshape(GROUPS, LANES),
        out_weight,
    )
    return (halves[0].astype(f32) + halves[1].astype(f32)).astype(bf16)


def solution(mesh):
    in_specs = (
        P(None, "ctx", "tp"),
        P(None, None, "tp"),
        P("tp", None),
        P("tp", None),
        P("tp"),
        P(("tp", "ctx"), None),
    )
    out_specs = P("ctx", "tp")
    return jax.shard_map(
        on_device, mesh=mesh, in_specs=in_specs, out_specs=out_specs, check_vma=False
    )
```
